256 devices in a mesh: ctx: 64 (over z, y, core), kv: 4 (over x).
Axes of the slice: x: 4, y: 4, z: 8, core: 2. Of those that a mesh axis runs over, the one named last changes fastest.
Arguments:
- query: bfloat16 [2, 8192, 8192], P(None, 'ctx', 'kv')
- kv_rows: bfloat16 [2, 8192, 2048], P(None, 'ctx', 'kv')
- keep: int32 [2, 64, 8, 512], P(None, 'ctx', 'kv'), may hold values from 0 to 639, as said below
- dest: int32 [65536, 1], P('ctx'), may hold values from 0 to 255; in each aligned block of 1024 rows (0 to 1023, 1024 to 2047, ...) at most 8 rows name the same one
- offsets: int32 [2], replicated, may hold values from 0 to 62, as said below
Outputs:
- attention: bfloat16 [2, 8192, 8192], P(None, 'ctx', 'kv')
- row_scores: float32 [2, 8, 40960], P(None, 'kv', 'ctx')
- owner_cache: bfloat16 [131072, 2048], P(('ctx', 'kv'))
The draws below stay inside these ranges and needn't reach their ends.
Inputs may be any that keep to these rules, and one draw needn't show every extreme that they name: `keep`: each list holds 512 distinct indices in increasing order; an index below 512 names a cache slot, an index k of 512 or more names span row k - 512. `dest`: among the 1024 rows of one context shard no owner is named more than 8 times; owner o is the device at position o in the ctx-major order of ctx and kv. `offsets`: one prompt starts at the first shard and another prompt at the second-to-last shard.
All inputs are finite; a program needn't handle non-finite values.
Results may differ from the reference program's by a relative error of at most 0.0049.
Values may be sent and summed in bfloat16 or wider, within the bound.
A program may use at most 192 MiB of HBM per device.

```python
import math
import jax
import jax.numpy as jnp
import numpy as np
from jax import lax

Q_HEADS = 64
KV_HEADS = 8
HEAD = 128
PROMPTS = 2
CH = 128
KEPT_ROWS = 512
TOKENS = 8192
OWNERS = 256
CAP = 8


def draw_query(key, part):
    shape = (PROMPTS, TOKENS, Q_HEADS * HEAD)
    own = jax.random.fold_in(key, 11)
    return jnp.clip(jax.random.normal(own, shape, jnp.float32), -6.0, 6.0).astype(jnp.bfloat16)


def draw_kv_rows(key, part):
    shape = (PROMPTS, TOKENS, KV_HEADS, 2 * HEAD)
    own = jax.random.fold_in(key, 21)
    base = jnp.clip(jax.random.normal(own, shape, jnp.float32), -6.0, 6.0)
    return base.reshape(PROMPTS, TOKENS, KV_HEADS * 2 * HEAD).astype(jnp.bfloat16)


def draw_keep(key, part):
    total_count = KEPT_ROWS + CH
    shards = TOKENS // CH
    unscaled_scores = jax.random.randint(jax.random.fold_in(key, 31), (PROMPTS, shards, KV_HEADS, total_count), 0, 4096)
    row_index = jnp.arange(total_count, dtype=jnp.int32)
    score_boost = jnp.where(row_index < KEPT_ROWS, 2048, 0)
    attention_scores = (unscaled_scores + score_boost) * total_count + row_index
    chosen = lax.top_k(attention_scores, KEPT_ROWS)[1]
    return jnp.sort(chosen, axis=-1).astype(jnp.int32)


def draw_offsets(key, part):
    shards = TOKENS // CH
    drawn = jax.random.randint(jax.random.fold_in(key, 41), (PROMPTS,), 0, shards - 1)
    order = jax.random.permutation(jax.random.fold_in(key, 42), PROMPTS)
    prompt_ids = jnp.arange(PROMPTS, dtype=jnp.int32)
    earliest = prompt_ids == order[0]
    latest = prompt_ids == order[1]
    result = jnp.where(earliest, 0, jnp.where(latest, shards - 2, drawn))
    return result.astype(jnp.int32)


def shared_out(stream_key, own, number, rows, count, top, reach, skew):
    ranking = jax.random.permutation(stream_key, count)
    heavy_load, usual = portions_of(count, rows * top, reach, skew, True), portions_of(count, rows * top, reach, skew, False)
    places = jnp.arange(count)

    def named(tallies, turn):
        used = int((tallies > 0).sum())
        fixed = max(1, used // 4)
        shifted = fixed + (places - fixed + turn * (used - fixed)) % max(1, count - fixed)
        return jnp.zeros((count,), jnp.int32).at[ranking[jnp.where(places < fixed, places, shifted)]].set(jnp.asarray(tallies, jnp.int32))

    tallies = jnp.where(number % 4 == 0, named(heavy_load, number // 4), named(usual, number - number // 4 - 1))
    mixed = jax.random.permutation(jax.random.fold_in(own, 3), count)
    source_of, receiver = mixed[0:count // 2 * 2:2], mixed[1:count // 2 * 2:2]
    slack = jnp.minimum(tallies[source_of] - 1, reach - tallies[receiver]) // 2
    slack = jnp.where((source_of == ranking[0]) | (receiver == ranking[0]) | (tallies[receiver] == 0), 0, jnp.maximum(slack, 0))
    shifted = jax.random.randint(jax.random.fold_in(own, 4), (count // 2,), 0, 1 << 20) % (slack + 1)
    tallies = tallies.at[source_of].add(-shifted).at[receiver].add(shifted)
    items = jnp.searchsorted(jnp.cumsum(tallies), jnp.arange(rows * top), side="right").astype(jnp.int32)
    listing = items.reshape(top, rows).T
    listing = listing[jax.random.permutation(jax.random.fold_in(own, 1), rows)]
    turn = jax.random.randint(jax.random.fold_in(own, 2), (rows, 1), 0, top)
    return jnp.take_along_axis(listing, (jnp.arange(top)[None, :] + turn) % top, axis=1)


def portions_of(number_of, total, bound, lean, full):
    portions = [(1 << 20) // math.isqrt(grade ** lean) + 1 for grade in range(1, number_of + 1)]
    largest = bound if full else min(bound, max(-(-total // number_of), total * portions[0] // sum(portions)))
    least = 1 if total - largest >= number_of - 1 else 0
    given, rest = [largest] + [least] * (number_of - 1), total - largest - least * (number_of - 1)
    while rest > 0:
        movable = [i for i in range(1, number_of) if given[i] < largest] or [i for i in range(1, number_of) if given[i] < bound]
        whole, remaining = sum([portions[i] for i in movable]), rest
        for i in movable:
            addition = min(bound - given[i], max(1, remaining * portions[i] // whole), rest)
            given[i] = given[i] + addition
            rest = rest - addition
    return np.array(given)


def setup_inputs(seed: int = 0) -> dict:
    arg_keys = jax.random.split(jax.random.key(seed), 6)
    query = draw_query(jax.random.fold_in(arg_keys[5], 71), 0)
    kv_rows = draw_kv_rows(jax.random.fold_in(arg_keys[5], 71), 0)
    keep = draw_keep(jax.random.fold_in(arg_keys[5], 71), 0)
    dest_keys = jax.random.split(jax.random.fold_in(arg_keys[3], 1), (TOKENS // CH * PROMPTS * KEPT_ROWS) // (PROMPTS * KEPT_ROWS))
    dest_turns = jax.random.permutation(jax.random.fold_in(arg_keys[3], 3), (TOKENS // CH * PROMPTS * KEPT_ROWS) // (PROMPTS * KEPT_ROWS))
    dest = jax.vmap(lambda own, number: shared_out(jax.random.fold_in(arg_keys[3], 2), own, number, PROMPTS * KEPT_ROWS, OWNERS, 1, CAP, 1))(dest_keys, dest_turns).reshape((TOKENS // CH * PROMPTS * KEPT_ROWS, 1))
    offsets = draw_offsets(jax.random.fold_in(arg_keys[5], 71), 0)
    return {"query": query, "kv_rows": kv_rows, "keep": keep, "dest": dest, "offsets": offsets}


def reference(query, kv_rows, keep, dest, offsets):
    group = Q_HEADS // KV_HEADS
    shards = TOKENS // CH
    width = 2 * HEAD
    qsix = query.reshape(PROMPTS, shards, CH, KV_HEADS, group, HEAD)
    kvfive = kv_rows.reshape(PROMPTS, shards, CH, KV_HEADS, width)
    scale = 1.0 / math.sqrt(HEAD)
    causal = jnp.arange(CH)[None, :] <= jnp.arange(CH)[:, None]
    highest = lax.Precision.HIGHEST

    def shard(carry, row_index):
        cache, valid = carry
        queries = lax.dynamic_index_in_dim(qsix, row_index, 1, keepdims=False).astype(jnp.float32)
        span_kv = lax.dynamic_index_in_dim(kvfive, row_index, 1, keepdims=False)
        rows_all = jnp.concatenate([cache, span_kv], axis=1)
        keys = rows_all[..., :HEAD].astype(jnp.float32)
        values = rows_all[..., HEAD:].astype(jnp.float32)
        attention_scores = jnp.einsum('pqhgd,pkhd->phgqk', queries, keys, precision=highest) * scale
        seen = jnp.broadcast_to(valid[:, :, None, :], (PROMPTS, KV_HEADS, CH, KEPT_ROWS))
        near = jnp.broadcast_to(causal[None, None], (PROMPTS, KV_HEADS, CH, CH))
        allowed = jnp.concatenate([seen, near], axis=3)[:, :, None]
        attention_scores = jnp.where(allowed, attention_scores, -1e+30)
        peak = lax.optimization_barrier(jnp.max(attention_scores, axis=-1, keepdims=True))
        expo = jnp.where(allowed, jnp.exp(attention_scores - peak), 0.0)
        weights = expo / lax.optimization_barrier(jnp.sum(expo, axis=-1, keepdims=True))
        rounded = lax.optimization_barrier(weights.astype(jnp.bfloat16)).astype(jnp.float32)
        mixed = jnp.einsum('phgqk,pkhd->pqhgd', rounded, values, precision=highest)
        flag = (row_index >= offsets).astype(jnp.float32)
        mixed = (mixed * flag[:, None, None, None, None]).astype(jnp.bfloat16)
        mass = lax.optimization_barrier(jnp.sum(weights, axis=(2, 3))) * flag[:, None, None]
        keep_now = lax.dynamic_index_in_dim(keep, row_index, 1, keepdims=False)
        picked = jnp.take_along_axis(rows_all, jnp.transpose(keep_now, (0, 2, 1))[..., None], axis=1)
        valid_all = jnp.concatenate([valid, jnp.ones((PROMPTS, KV_HEADS, CH), dtype=bool)], axis=2)
        new_valid = jnp.take_along_axis(valid_all, keep_now, axis=2)
        living = flag > 0.5
        cache = jnp.where(living[:, None, None, None], picked, cache)
        valid = jnp.where(living[:, None, None], new_valid, valid)
        return ((cache, valid), (mixed, mass, cache))
    start = (jnp.zeros((PROMPTS, KEPT_ROWS, KV_HEADS, width), jnp.bfloat16), jnp.zeros((PROMPTS, KV_HEADS, KEPT_ROWS), dtype=bool))
    _, (mixed, mass, caches) = lax.scan(shard, start, jnp.arange(shards, dtype=jnp.int32))
    attention = jnp.transpose(mixed, (1, 0, 2, 3, 4, 5)).reshape(PROMPTS, TOKENS, Q_HEADS * HEAD)
    row_scores = jnp.transpose(mass, (1, 2, 0, 3)).reshape(PROMPTS, KV_HEADS, shards * (KEPT_ROWS + CH))
    rows = caches.reshape(shards, PROMPTS * KEPT_ROWS, KV_HEADS * width)
    owning_shards = dest.reshape(shards, PROMPTS * KEPT_ROWS)
    onehot = (owning_shards[..., None] == jnp.arange(OWNERS, dtype=jnp.int32)).astype(jnp.int32)
    rank = lax.optimization_barrier(jnp.sum((jnp.cumsum(onehot, axis=1) - 1) * onehot, axis=2))
    source = jnp.arange(shards, dtype=jnp.int32)[:, None]
    flat = (owning_shards * shards + source) * CAP + rank
    owner_cache = jnp.zeros((OWNERS * shards * CAP, KV_HEADS * width), jnp.bfloat16)
    owner_cache = owner_cache.at[flat.reshape(-1)].set(rows.reshape(-1, KV_HEADS * width))
    return (attention, row_scores, owner_cache)
```

```python
import functools, math
import jax, jax.numpy as jnp
from jax import lax
from jax.sharding import PartitionSpec as P
from jax.experimental import pallas as pl
from jax.experimental.pallas import tpu as pltpu
MESH = pl.DeviceIdType.MESH
BF = jnp.bfloat16
HEAD = 128

def lookup(table, index):
    row = lax.broadcasted_iota(jnp.int32, (8, 128), 0)
    lane = jnp.bitwise_and(index, 127)
    part = jnp.right_shift(index, 7)
    out = jnp.zeros_like(table)
    for k in range(4):
        low = jnp.broadcast_to(table[k : k + 1], (8, 128))
        high = jnp.broadcast_to(table[4 + k : 5 + k], (8, 128))
        spread = jnp.where(row < 4, low, high)
        found = jnp.take_along_axis(spread, lane, axis=1, mode="promise_in_bounds")
        out = jnp.where(part == k, found, out)
    return out

def picker(index, count):
    rows = lax.broadcasted_iota(jnp.int32, (count, 128), 0)
    return jnp.where(rows == index, 1.0, 0.0).astype(BF)

def dot(a, b):
    return jnp.dot(a, b, preferred_element_type=jnp.float32)

def k1(kv_ref, keep_ref, late_ref, latekeep_ref, in_ref, valid_ref, spans, keeps, own, owns, marks, cz, lspan, lkeep,
       ssp, ske, sow, sma, scz, rsp, rke, row_, rma, rcz, sl, rl):
    j = lax.axis_index("ctx"); x = lax.axis_index("kv")
    z = j // 8; i = lax.rem(j, 8)
    def zdev(zz): return (zz * 8 + i, x)
    def pdev(ii): return (z * 8 + ii, x)
    barrier = pltpu.get_barrier_semaphore()
    for k in range(1, 8):
        pl.semaphore_signal(barrier, inc=1, device_id=pdev(lax.rem(i + k, 8)), device_id_type=MESH)
        pl.semaphore_signal(barrier, inc=1, device_id=zdev(lax.rem(z + k, 8)), device_id_type=MESH)
    keeps[i] = keep_ref[...]
    for b in range(4):
        spans[i, b * 128 : (b + 1) * 128, :] = kv_ref[b].T
    pl.semaphore_wait(barrier, 14)
    def send(src, dst, ss, rs, dev):
        return pltpu.make_async_remote_copy(src_ref=src, dst_ref=dst, send_sem=ss, recv_sem=rs, device_id=dev, device_id_type=MESH)
    plane = []
    for k in range(1, 8):
        c = send(keeps.at[i], keeps.at[i], ske.at[k], rke.at[i], pdev(lax.rem(i + k, 8))); c.start(); plane.append(c)
    for k in range(1, 8):
        c = send(spans.at[i], spans.at[i], ssp.at[k], rsp.at[i], pdev(lax.rem(i + k, 8))); c.start(); plane.append(c)
    @pl.when(j == 62)
    def _():
        for b in range(4):
            lspan[b * 128 : (b + 1) * 128, :] = late_ref[b].T
        lkeep[...] = latekeep_ref[...]
        send(lkeep, lkeep, sl.at[0], rl.at[0], (63, x)).start()
        send(lspan, lspan, sl.at[1], rl.at[1], (63, x)).start()
    def arrive(buf, sem, k):
        pltpu.make_async_copy(buf.at[k], buf.at[k], sem.at[k]).wait()
    for k in range(1, 8):
        arrive(keeps, rke, lax.rem(i + k, 8))
    slot = lax.rem(lax.broadcasted_iota(jnp.int32, (8, 128), 0), 4) * 128 + lax.broadcasted_iota(jnp.int32, (8, 128), 1)
    pre = slot; mine = slot
    for n in range(8):
        mine = jnp.where(i == n, pre, mine)
        kept = keeps[n]
        pre = jnp.where(kept < 512, lookup(pre, jnp.minimum(kept, 511)), kept + 128 * n)
    marks[z] = pre
    for k in range(1, 8):
        @pl.when(z + k < 8)
        def _():
            send(marks.at[z], marks.at[z], sma.at[k], rma.at[z], zdev(z + k)).start()
    for k in range(1, 8):
        arrive(spans, rsp, lax.rem(i + k, 8))
    cols = pl.ds(pl.multiple_of(i * 64, 64), 64)
    head = jnp.where(i < 4, pre[0:4], pre[4:8])
    unit = jnp.concatenate([spans[n, cols, :] for n in range(8)], axis=1)
    for k in range(4):
        own[k * 64 : (k + 1) * 64, :] = dot(unit, picker(head[k : k + 1] - 512, 1024)).astype(BF)
    for k in range(1, 8):
        @pl.when(z + k < 8)
        def _():
            send(own, owns.at[z], sow.at[k], row_.at[z], zdev(z + k)).start()
    for h in range(2):
        table = jnp.concatenate([spans[n, h * 256 : (h + 1) * 256, :] for n in range(8)], axis=1)
        for k in range(4):
            in_ref[0, k, h * 256 : (h + 1) * 256, :] = dot(table, picker(mine[h * 4 + k : h * 4 + k + 1] - 512, 1024)).astype(BF)
    @pl.when(j != 63)
    def _():
        in_ref[1] = jnp.zeros((4, 512, 128), BF)
        valid_ref[1] = jnp.zeros((8, 128), jnp.int32)
    @pl.when(j == 63)
    def _():
        pltpu.make_async_copy(lkeep, lkeep, rl.at[0]).wait()
        pltpu.make_async_copy(lspan, lspan, rl.at[1]).wait()
        kept = lkeep[...]
        valid_ref[1] = jnp.where(kept >= 512, 1, 0)
        for h in range(2):
            for k in range(4):
                in_ref[1, k, h * 256 : (h + 1) * 256, :] = dot(lspan[h * 256 : (h + 1) * 256, :], picker(kept[h * 4 + k : h * 4 + k + 1] - 512, 128)).astype(BF)
    for n in range(7):
        @pl.when(n < z)
        def _():
            arrive(marks, rma, n)
    cur = jnp.full((8, 128), -1, jnp.int32)
    for n in range(7):
        m = jnp.where(n < z, marks[n], slot)
        new = jnp.where(m < 512, lookup(cur, jnp.minimum(m, 511)), n * 512 + slot)
        cur = jnp.where(n < z, new, cur)
    chead = jnp.where(i < 4, cur[0:4], cur[4:8])
    acc_ref = cz.at[i]
    acc_ref[...] = jnp.zeros((256, 128), BF)
    for n in range(7):
        @pl.when(n < z)
        def _():
            arrive(owns, row_, n)
            table = jnp.concatenate([owns[n, q * 64 : (q + 1) * 64, :] for q in range(4)], axis=1)
            for k in range(4):
                acc_ref[k * 64 : (k + 1) * 64, :] += dot(table, picker(chead[k : k + 1] - n * 512, 512)).astype(BF)
    for k in range(1, 8):
        c = send(cz.at[i], cz.at[i], scz.at[k], rcz.at[i], pdev(lax.rem(i + k, 8))); c.start(); plane.append(c)
    was = jnp.where(cur >= 0, 1, 0)
    valid_ref[0] = jnp.where(mine >= 512, 1, lookup(was, jnp.minimum(mine, 511)))
    for k in range(1, 8):
        arrive(cz, rcz, lax.rem(i + k, 8))
    for h in range(2):
        table = jnp.concatenate(
            [jnp.concatenate([cz[n, q * 64 : (q + 1) * 64, :] for q in range(4)], axis=1) for n in range(h * 4, h * 4 + 4)], axis=0
        )
        for k in range(4):
            in_ref[0, k, h * 256 : (h + 1) * 256, :] += dot(table, picker(mine[h * 4 + k : h * 4 + k + 1], 512)).astype(BF)
    for c in plane:
        c.wait_send()
    for k in range(1, 8):
        @pl.when(z + k < 8)
        def _():
            send(marks.at[z], marks.at[z], sma.at[k], rma.at[z], zdev(z + k)).wait_send()
            send(own, owns.at[z], sow.at[k], row_.at[z], zdev(z + k)).wait_send()
    @pl.when(j == 62)
    def _():
        send(lkeep, lkeep, sl.at[0], rl.at[0], (63, x)).wait_send()
        send(lspan, lspan, sl.at[1], rl.at[1], (63, x)).wait_send()

def handed_on(kv_e, keep_e, kv_l, keep_l):
    V = pltpu.VMEM; S = pltpu.SemaphoreType.DMA
    return pl.pallas_call(k1,
        out_shape=(jax.ShapeDtypeStruct((2, 4, 512, 128), BF), jax.ShapeDtypeStruct((2, 8, 128), jnp.int32)),
        in_specs=[pl.BlockSpec(memory_space=V)] * 4, out_specs=(pl.BlockSpec(memory_space=V),) * 2,
        scratch_shapes=[V((8, 512, 128), BF), V((8, 8, 128), jnp.int32), V((256, 128), BF), V((8, 256, 128), BF),
                        V((8, 8, 128), jnp.int32), V((8, 256, 128), BF), V((512, 128), BF), V((8, 128), jnp.int32)]
                       + [S((8,))] * 10 + [S((2,))] * 2,
        compiler_params=pltpu.CompilerParams(collective_id=0, has_side_effects=True, vmem_limit_bytes=32 << 20),
    )(kv_e, keep_e, kv_l, keep_l)


def placed_rows(owner_ids, capacity):
    count = owner_ids.shape[0]
    before = jnp.arange(count)[None, :] < jnp.arange(count)[:, None]
    same = owner_ids[None, :] == owner_ids[:, None]
    rank = jnp.sum(jnp.where(before & same, 1, 0), axis=1)
    return owner_ids * capacity + rank


def local(query, kv_rows, keep, dest, offsets):
    prompts, span, qwidth = query.shape
    position = lax.axis_index("ctx")
    first = offsets[0] == 0
    keep_local = keep[:, 0]
    tiles = keep_local.reshape(2, 8, 128)
    blocks = jnp.transpose(kv_rows.reshape(2, span, 4, 128), (0, 2, 1, 3))
    in_t, in_valid = handed_on(
        jnp.where(first, blocks[0], blocks[1]),
        jnp.where(first, tiles[0], tiles[1]),
        jnp.where(first, blocks[1], blocks[0]),
        jnp.where(first, tiles[1], tiles[0]),
    )
    in_t = jnp.where(first, in_t, in_t[::-1])
    in_t = jnp.transpose(in_t, (0, 2, 1, 3)).reshape(2, 2, 256, 512)
    valid = jnp.where(first, in_valid, in_valid[::-1]).reshape(2, 2, 512) > 0
    active = position >= offsets
    span_t = jnp.transpose(kv_rows.reshape(2, span, 2, 256), (0, 2, 3, 1))
    all_t = jnp.concatenate([in_t, span_t], axis=3)
    chosen = jnp.where(active[:, None, None], keep_local, jnp.arange(512, dtype=jnp.int32))
    pick = (chosen[..., None] == jnp.arange(640, dtype=jnp.int32)).astype(BF)
    outgoing = jnp.einsum("phst,phct->pshc", pick, all_t, preferred_element_type=jnp.float32).astype(BF)
    target = placed_rows(dest[:, 0], 8)
    placing = (target[None, :] == jnp.arange(2048, dtype=jnp.int32)[:, None]).astype(BF)
    packed = jnp.dot(placing, outgoing.reshape(1024, 512), preferred_element_type=jnp.float32).astype(BF)
    arrived = lax.all_to_all(packed.reshape(256, 8, 512), ("ctx", "kv"), 0, 0, tiled=True)
    owner_cache = jnp.transpose(arrived.reshape(64, 4, 8, 512), (0, 2, 1, 3)).reshape(512, 2048)
    qfive = query.reshape(2, span, 2, 8, HEAD)
    causal = jnp.arange(span)[None, :] <= jnp.arange(span)[:, None]
    scale = 1.0 / math.sqrt(HEAD)
    outputs, masses = [], []
    for prompt in range(2):
        flag = active[prompt].astype(jnp.float32)
        for head in range(2):
            table = all_t[prompt, head]
            scores = jnp.einsum("qgd,dk->gqk", qfive[prompt, :, head], table[:HEAD], preferred_element_type=jnp.float32) * scale
            seen = jnp.broadcast_to(valid[prompt, head][None, :], (span, 512))
            allowed = jnp.concatenate([seen, causal], axis=1)[None]
            scores = jnp.where(allowed, scores, -1e30)
            peak = jnp.max(scores, axis=-1, keepdims=True)
            expo = jnp.where(allowed, jnp.exp(scores - peak), 0.0)
            weights = expo / jnp.sum(expo, axis=-1, keepdims=True)
            mixed = jnp.einsum("gqk,dk->qgd", weights.astype(BF), table[HEAD:], preferred_element_type=jnp.float32)
            outputs.append((mixed * flag).astype(BF))
            masses.append(jnp.sum(weights, axis=(0, 1)) * flag)
    attention = jnp.stack(outputs).reshape(2, 2, span, 8 * HEAD).transpose(0, 2, 1, 3).reshape(2, span, qwidth)
    return (attention, jnp.stack(masses).reshape(2, 2, 640), owner_cache)


def solution(mesh):
    placed = (
        P(None, "ctx", "kv"),
        P(None, "ctx", "kv"),
        P(None, "ctx", "kv", None),
        P("ctx", None),
        P(),
    )
    return jax.shard_map(
        local,
        mesh=mesh,
        in_specs=placed,
        out_specs=(P(None, "ctx", "kv"), P(None, "kv", "ctx"), P(("ctx", "kv"), None)),
        check_vma=False,
    )
```

```python
import math

import jax
import jax.numpy as jnp
from jax import lax
from jax.experimental import pallas as pl
from jax.experimental.pallas import tpu as pltpu
from jax.sharding import PartitionSpec as P

MESH = pl.DeviceIdType.MESH
BF = jnp.bfloat16
HEAD = 128


def lookup(table, index):
    row = lax.broadcasted_iota(jnp.int32, (8, 128), 0)
    lane = jnp.bitwise_and(index, 127)
    part = jnp.right_shift(index, 7)
    out = jnp.zeros_like(table)
    for k in range(4):
        low = jnp.broadcast_to(table[k : k + 1], (8, 128))
        high = jnp.broadcast_to(table[4 + k : 5 + k], (8, 128))
        spread = jnp.where(row < 4, low, high)
        found = jnp.take_along_axis(spread, lane, axis=1, mode="promise_in_bounds")
        out = jnp.where(part == k, found, out)
    return out


def picker(index, count):
    rows = lax.broadcasted_iota(jnp.int32, (count, 128), 0)
    return jnp.where(rows == index, 1.0, 0.0).astype(BF)


def dot(a, b):
    return jnp.dot(a, b, preferred_element_type=jnp.float32)


def dot_t(a, b):
    return lax.dot_general(a, b, (((1,), (1,)), ((), ())), preferred_element_type=jnp.float32)


def lanes(parts):
    return jnp.concatenate(parts, axis=1)


def inverse(kept, values):
    row = lax.broadcasted_iota(jnp.int32, (16, 128), 0)
    total = jnp.zeros((16, 640), jnp.float32)
    for k in range(4):
        value = values[k : k + 1] + 1
        high = jnp.broadcast_to(jnp.right_shift(value, 6), (16, 128))
        low = jnp.broadcast_to(jnp.bitwise_and(value, 63), (16, 128))
        digits = jnp.where(row == 0, high, jnp.where(row == 1, low, 0)).astype(jnp.float32).astype(BF)
        total = total + dot_t(digits, picker(kept[k : k + 1], 640))
    return (total[0:1] * 64.0 + total[1:2]).astype(jnp.int32) - 1


def half(rows, which):
    return jnp.where(which == 0, rows[0:4], rows[4:8])


def kernel(offs, kv, q, keep, goal, attn, mass, recv, spans, keeps, own, owns, marks, cz, late, cache, valid, tab, metas, tabl, obuf,
           s_sp, s_ke, s_ow, s_ma, s_cz, r_sp, r_ke, r_ow, r_ma, r_cz, s_la, r_la,
           s_up, r_up, s_dn, r_dn, s_mu, r_mu, s_md, r_md, s_lu, r_lu, s_ld, r_ld, s_ex, r_ex, s_lo):
    j = lax.axis_index("ctx")
    x = lax.axis_index("kv")
    z = j // 8
    i = lax.rem(j, 8)
    y = i // 2
    c = lax.rem(i, 2)
    me = i * 4 + x
    early = jnp.where(offs[0] == 0, 0, 1)

    def zdev(n):
        return (n * 8 + i, x)

    def pdev(n):
        return (z * 8 + n, x)

    def mdev(n):
        return (z * 8 + n // 4, lax.rem(n, 4))

    barrier = pltpu.get_barrier_semaphore()

    @pl.loop(1, 32)
    def _(k):
        pl.semaphore_signal(barrier, inc=1, device_id=mdev(lax.rem(me + k, 32)), device_id_type=MESH)

    @pl.loop(1, 8)
    def _(k):
        pl.semaphore_signal(barrier, inc=1, device_id=zdev(lax.rem(z + k, 8)), device_id_type=MESH)

    keeps[i, 0:8, :] = keep[early]
    keeps[i, 8:16, :] = keep[1 - early]
    keeps[i, 16:20, :] = goal[early]
    keeps[i, 20:24, :] = goal[1 - early]
    for b in range(4):
        spans[i, b * 128 : (b + 1) * 128, :] = kv[early, b].T
    final_pair = j >= 62

    @pl.when(final_pair)
    def _():
        for b in range(4):
            late[c, b * 128 : (b + 1) * 128, :] = kv[1 - early, b].T

    pl.semaphore_wait(barrier, 38)

    def send(src, dst, ss, rs, dev):
        return pltpu.make_async_remote_copy(
            src_ref=src, dst_ref=dst, send_sem=ss, recv_sem=rs, device_id=dev, device_id_type=MESH
        )

    def took(view, sem):
        pltpu.make_async_copy(view, view, sem).wait()

    def arrive(buf, sem, k):
        took(buf.at[k], sem.at[k])

    def late_copy():
        return send(late.at[c], late.at[c], s_la, r_la, pdev(7 - c))

    waits = []
    for k in range(1, 8):
        copy = send(keeps.at[i], keeps.at[i], s_ke.at[k], r_ke.at[i], pdev(lax.rem(i + k, 8)))
        copy.start()
        waits.append(copy)
    for k in range(1, 8):
        copy = send(spans.at[i], spans.at[i], s_sp.at[k], r_sp.at[i], pdev(lax.rem(i + k, 8)))
        copy.start()
        waits.append(copy)

    @pl.when(final_pair)
    def _():
        late_copy().start()

    for k in range(1, 8):
        arrive(keeps, r_ke, lax.rem(i + k, 8))
    slot = lax.rem(lax.broadcasted_iota(jnp.int32, (8, 128), 0), 4) * 128 + lax.broadcasted_iota(jnp.int32, (8, 128), 1)
    pre, mine = slot, slot
    for n in range(8):
        mine = jnp.where(i == n, pre, mine)
        kept = keeps[n, 0:8, :]
        pre = jnp.where(kept < 512, lookup(pre, jnp.minimum(kept, 511)), kept + 128 * n)
    marks[z] = pre

    def marks_copy(k):
        return send(marks.at[z], marks.at[z], s_ma.at[k], r_ma.at[z], zdev(z + k))

    def own_copy(k):
        return send(own, owns.at[z], s_ow.at[k], r_ow.at[z], zdev(z + k))

    for k in range(1, 8):
        @pl.when(z + k < 8)
        def _():
            marks_copy(k).start()

    first, second = i - c, i - c + 1
    goal0 = keeps[first, 16:20, :]
    goal1 = inverse(half(keeps[second, 0:8, :], c), keeps[second, 16:20, :])
    metas[z, 0:4, :] = goal0
    metas[z, 4:8, :] = jnp.full((4, 128), -1, jnp.int32)
    for k in range(5):
        metas[z, 8 + k : 9 + k, :] = goal1[:, k * 128 : (k + 1) * 128]
    metas[z, 13:16, :] = jnp.full((3, 128), -1, jnp.int32)

    @pl.when(final_pair)
    def _():
        kept0 = half(keeps[first, 8:16, :], c)
        kept1 = half(keeps[second, 8:16, :], c)
        out1 = inverse(kept1, keeps[second, 20:24, :])
        back = jnp.concatenate([out1[:, k * 128 : (k + 1) * 128] for k in range(4)], axis=0)
        metas[z, 5:6, :] = inverse(kept0, keeps[first, 20:24, :])[:, 512:640]
        metas[z, 13:14, :] = inverse(kept0, back)[:, 512:640]
        metas[z, 14:15, :] = out1[:, 512:640]

    for k in range(1, 8):
        arrive(spans, r_sp, lax.rem(i + k, 8))
    cols = pl.ds(pl.multiple_of(i * 64, 64), 64)
    head = jnp.where(i < 4, pre[0:4], pre[4:8])
    unit = lanes([spans[n, cols, :] for n in range(8)])
    for k in range(4):
        own[k * 64 : (k + 1) * 64, :] = dot(unit, picker(head[k : k + 1] - 512, 1024)).astype(BF)
    for k in range(1, 8):
        @pl.when(z + k < 8)
        def _():
            own_copy(k).start()

    for h in range(2):
        table = lanes([spans[n, h * 256 : (h + 1) * 256, :] for n in range(8)])
        for k in range(4):
            cache[0, k, h * 256 : (h + 1) * 256, :] = dot(table, picker(mine[h * 4 + k : h * 4 + k + 1] - 512, 1024)).astype(BF)

    for n in range(7):
        @pl.when(n < z)
        def _():
            arrive(marks, r_ma, n)
    cur = jnp.full((8, 128), -1, jnp.int32)
    for n in range(7):
        m = jnp.where(n < z, marks[n], slot)
        new = jnp.where(m < 512, lookup(cur, jnp.minimum(m, 511)), n * 512 + slot)
        cur = jnp.where(n < z, new, cur)
    chead = jnp.where(i < 4, cur[0:4], cur[4:8])
    part = cz.at[i]
    part[...] = jnp.zeros((256, 128), BF)
    for n in range(7):
        @pl.when(n < z)
        def _():
            arrive(owns, r_ow, n)
            table = lanes([owns[n, p * 64 : (p + 1) * 64, :] for p in range(4)])
            for k in range(4):
                part[k * 64 : (k + 1) * 64, :] += dot(table, picker(chead[k : k + 1] - n * 512, 512)).astype(BF)
    for k in range(1, 8):
        copy = send(cz.at[i], cz.at[i], s_cz.at[k], r_cz.at[i], pdev(lax.rem(i + k, 8)))
        copy.start()
        waits.append(copy)
    was = jnp.where(cur >= 0, 1, 0)
    valid[0] = jnp.where(mine >= 512, 1, lookup(was, jnp.minimum(mine, 511)))

    @pl.when(final_pair)
    def _():
        took(late.at[1 - c], r_la)
        for h in range(2):
            tabl[h] = late[h, pl.ds(pl.multiple_of(c * 256, 256), 256), :]

    for k in range(1, 8):
        arrive(cz, r_cz, lax.rem(i + k, 8))
    for h in range(2):
        table = jnp.concatenate(
            [lanes([cz[n, p * 64 : (p + 1) * 64, :] for p in range(4)]) for n in range(h * 4, h * 4 + 4)], axis=0
        )
        for k in range(4):
            cache[0, k, h * 256 : (h + 1) * 256, :] += dot(table, picker(mine[h * 4 + k : h * 4 + k + 1], 512)).astype(BF)

    tab[z, 4] = spans[second, pl.ds(pl.multiple_of(c * 256, 256), 256), :]

    @pl.when(c == 1)
    def _():
        for k in range(4):
            tab[z, k] = cache[0, k, 256:512, :]

    @pl.when(c == 0)
    def _():
        table = lanes([cache[0, k, 0:256, :] for k in range(4)] + [spans[i, 0:256, :]])
        kept = keeps[i, 0:8, :]
        for k in range(4):
            tab[z, k] = dot(table, picker(kept[k : k + 1], 640)).astype(BF)

    above, below = zdev(lax.rem(z + 1, 8)), zdev(lax.rem(z + 7, 8))

    def up(s):
        o = lax.rem(z + 9 - s, 8)
        view = tab.at[o, pl.ds(0, 5 if s < 4 else 2)]
        return o, [
            send(metas.at[o], metas.at[o], s_mu.at[s], r_mu.at[s], above),
            send(view, view, s_up.at[s], r_up.at[s], above),
        ], send(tabl, tabl, s_lu, r_lu, above)

    def down(s):
        o = lax.rem(z + s - 1, 8)
        view = tab.at[o, pl.ds(0, 5)] if s < 4 else tab.at[o, pl.ds(2, 3)]
        parts = [send(view, view, s_dn.at[s], r_dn.at[s], below)]
        if s < 4:
            parts.append(send(metas.at[o], metas.at[o], s_md.at[s], r_md.at[s], below))
        return o, parts, send(tabl, tabl, s_ld, r_ld, below) if s < 4 else None

    def pass_on(s):
        o, parts, extra = up(s)
        for copy in parts:
            copy.start()

        @pl.when((o == 7) & (y == 3))
        def _():
            extra.start()

        o, parts, extra = down(s)
        for copy in parts:
            copy.start()
        if s < 4:
            @pl.when((o == 7) & (y == 3))
            def _():
                extra.start()

    def passed(s):
        for make in (up, down):
            o, parts, extra = make(s)
            for copy in parts:
                copy.wait_send()
            if s < 4 or make is up:
                @pl.when((o == 7) & (y == 3))
                def _():
                    extra.wait_send()

    def receive(s):
        o = lax.rem(z + 8 - s, 8)
        took(metas.at[o], r_mu.at[s])
        took(tab.at[o, pl.ds(0, 5 if s < 4 else 2)], r_up.at[s])

        @pl.when((o == 7) & (y == 3))
        def _():
            took(tabl, r_lu)

        o = lax.rem(z + s, 8)
        took(tab.at[o, pl.ds(0, 5)] if s < 4 else tab.at[o, pl.ds(2, 3)], r_dn.at[s])
        if s < 4:
            took(metas.at[o], r_md.at[s])

            @pl.when((o == 7) & (y == 3))
            def _():
                took(tabl, r_ld)

    def exchange(o, n):
        dst = recv.at[pl.ds(x * 4 + c * 2, 2), pl.ds(pl.multiple_of((o * 4 + y) * 16, 16), 16), :]
        return send(obuf.at[o, :, pl.ds(pl.multiple_of(n * 16, 16), 16), :], dst, s_ex.at[o], r_ex.at[o], mdev(n))

    def keep_local(o):
        dst = recv.at[pl.ds(x * 4 + c * 2, 2), pl.ds(pl.multiple_of((o * 4 + y) * 16, 16), 16), :]
        return pltpu.make_async_copy(obuf.at[o, :, pl.ds(pl.multiple_of(me * 16, 16), 16), :], dst, s_lo.at[o])

    line = lax.broadcasted_iota(jnp.int32, (512, 128), 0)
    place = z * 256 + jnp.right_shift(line, 4) * 8 + jnp.bitwise_and(line, 7)
    later = jnp.bitwise_and(line, 8) > 0

    def hit(o, k):
        wanted = jnp.where(later, metas[o, 8 + k : 9 + k, :], metas[o, k : k + 1, :])
        return jnp.where(wanted == place, 1.0, 0.0).astype(BF)

    def hand_out(o):
        rows = dot_t(lanes([hit(o, k) for k in range(5)]), lanes([tab[o, k] for k in range(5)])).astype(BF)
        obuf[o, 0] = rows[:, 0:128]
        obuf[o, 1] = rows[:, 128:256]

        @pl.when((o == 7) & (y == 3))
        def _():
            rows = dot_t(lanes([hit(o, k) for k in (5, 6)]), lanes([tabl[k] for k in range(2)])).astype(BF)
            obuf[o, 0] += rows[:, 0:128]
            obuf[o, 1] += rows[:, 128:256]

        @pl.loop(1, 32)
        def _(k):
            exchange(o, lax.rem(me + k, 32)).start()

        keep_local(o).start()

    own_tokens = lax.broadcasted_iota(jnp.int32, (128, 128), 1) <= lax.broadcasted_iota(jnp.int32, (128, 128), 0)

    def attend(p, h, span_t):
        def chunk(at):
            return lanes([cache[p, k, at : at + 128, :] for k in range(4)] + [span_t[at : at + 128, :]])

        keys, values = chunk(h * 256), chunk(h * 256 + 128)
        seen = lanes([jnp.broadcast_to(valid[p, h * 4 + k : h * 4 + k + 1, :], (128, 128)) for k in range(4)]) > 0
        near = own_tokens
        prompt = early if p == 0 else 1 - early
        scale = 1.0 / math.sqrt(HEAD)

        def one(g, total):
            scores = dot(q[prompt, h * 8 + g], keys) * scale
            old = jnp.where(seen, scores[:, 0:512], -1e30)
            new = jnp.where(near, scores[:, 512:640], -1e30)
            peak = jnp.maximum(jnp.max(old, axis=1, keepdims=True), jnp.max(new, axis=1, keepdims=True))
            expo = lanes([jnp.where(seen, jnp.exp(old - peak), 0.0), jnp.where(near, jnp.exp(new - peak), 0.0)])
            weights = expo * (1.0 / jnp.sum(expo, axis=1, keepdims=True))
            attn[p, h * 8 + g] = dot_t(weights.astype(BF), values).astype(BF)
            return total + jnp.sum(weights.reshape(16, 8, 640), axis=0)

        total = lax.fori_loop(0, 8, one, jnp.zeros((8, 640), jnp.float32))
        mass[p * 2 + h : p * 2 + h + 1, :] = jnp.sum(total, axis=0, keepdims=True)

    def attend_late():
        @pl.when(final_pair)
        def _():
            cache[1] = jnp.zeros((4, 512, 128), BF)
            valid[1] = jnp.zeros((8, 128), jnp.int32)

            @pl.when(c == 1)
            def _():
                kept = keeps[first, 8:16, :]
                valid[1] = jnp.where(kept >= 512, 1, 0)
                for h in range(2):
                    for k in range(4):
                        cache[1, k, h * 256 : (h + 1) * 256, :] = dot(
                            late[0, h * 256 : (h + 1) * 256, :], picker(kept[h * 4 + k : h * 4 + k + 1] - 512, 128)
                        ).astype(BF)

            for h in range(2):
                attend(1, h, late.at[c])

        @pl.when(jnp.logical_not(final_pair))
        def _():
            attn[1] = jnp.zeros((16, 128, 128), BF)
            mass[2:4, :] = jnp.zeros((2, 640), jnp.float32)

    pass_on(1)
    hand_out(z)
    attend(0, 0, spans.at[i])
    for s in (1, 2, 3):
        receive(s)
        pass_on(s + 1)
        hand_out(lax.rem(z + 8 - s, 8))
        hand_out(lax.rem(z + s, 8))
        if s == 1:
            attend(0, 1, spans.at[i])
        if s == 2:
            attend_late()
    receive(4)
    hand_out(lax.rem(z + 4, 8))

    for copy in waits:
        copy.wait_send()
    for k in range(1, 8):
        @pl.when(z + k < 8)
        def _():
            marks_copy(k).wait_send()
            own_copy(k).wait_send()

    @pl.when(final_pair)
    def _():
        late_copy().wait_send()

    for s in (1, 2, 3, 4):
        passed(s)

    @pl.loop(0, 8)
    def _(o):
        keep_local(o).wait()
        took(obuf.at[o, :, pl.ds(0, 496), :], s_ex.at[o])
        took(recv.at[pl.ds(0, 2), pl.ds(0, 496), :], r_ex.at[o])


def whole(offsets, kv, q, keep, goal):
    V, D = pltpu.VMEM, pltpu.SemaphoreType.DMA
    vmem = pl.BlockSpec(memory_space=V)
    return pl.pallas_call(
        kernel,
        out_shape=(
            jax.ShapeDtypeStruct((2, 16, 128, 128), BF),
            jax.ShapeDtypeStruct((4, 640), jnp.float32),
            jax.ShapeDtypeStruct((16, 512, 128), BF),
        ),
        in_specs=[pl.BlockSpec(memory_space=pltpu.SMEM)] + [vmem] * 4,
        out_specs=(vmem,) * 3,
        scratch_shapes=[
            V((8, 512, 128), BF),
            V((8, 24, 128), jnp.int32),
            V((256, 128), BF),
            V((8, 256, 128), BF),
            V((8, 8, 128), jnp.int32),
            V((8, 256, 128), BF),
            V((2, 512, 128), BF),
            V((2, 4, 512, 128), BF),
            V((2, 8, 128), jnp.int32),
            V((8, 5, 256, 128), BF),
            V((8, 16, 128), jnp.int32),
            V((2, 256, 128), BF),
            V((8, 2, 512, 128), BF),
        ]
        + [D((8,))] * 10
        + [D] * 2
        + [D((5,))] * 8
        + [D] * 4
        + [D((8,))] * 3,
        compiler_params=pltpu.CompilerParams(collective_id=0, has_side_effects=True, vmem_limit_bytes=40 << 20),
    )(offsets, kv, q, keep, goal)


def placed_rows(owner_ids, capacity):
    count = owner_ids.shape[0]
    before = jnp.arange(count)[None, :] < jnp.arange(count)[:, None]
    same = owner_ids[None, :] == owner_ids[:, None]
    rank = jnp.sum(jnp.where(before & same, 1, 0), axis=1)
    return owner_ids * capacity + rank


def local(query, kv_rows, keep, dest, offsets):
    span = query.shape[1]
    first = offsets[0] == 0
    attn, mass, owned = whole(
        offsets,
        jnp.transpose(kv_rows.reshape(2, span, 4, 128), (0, 2, 1, 3)),
        jnp.transpose(query.reshape(2, span, 16, 128), (0, 2, 1, 3)),
        keep.reshape(2, 8, 128),
        placed_rows(dest[:, 0], 8).reshape(2, 4, 128),
    )
    attn = jnp.where(first, attn, attn[::-1])
    attention = jnp.transpose(attn, (0, 2, 1, 3)).reshape(query.shape)
    mass = mass.reshape(2, 2, 640)
    row_scores = jnp.where(first, mass, mass[::-1])
    owner_cache = jnp.transpose(owned, (1, 0, 2)).reshape(512, 2048)
    return (attention, row_scores, owner_cache)


def solution(mesh):
    placed = (
        P(None, "ctx", "kv"),
        P(None, "ctx", "kv"),
        P(None, "ctx", "kv", None),
        P("ctx", None),
        P(),
    )
    return jax.shard_map(
        local,
        mesh=mesh,
        in_specs=placed,
        out_specs=(P(None, "ctx", "kv"), P(None, "kv", "ctx"), P(("ctx", "kv"), None)),
        check_vma=False,
    )
```

```python
import math

import jax
import jax.numpy as jnp
from jax import lax
from jax.experimental import pallas as pl
from jax.experimental.pallas import tpu as pltpu
from jax.sharding import PartitionSpec as P

MESH = pl.DeviceIdType.MESH
BF = jnp.bfloat16
HEAD = 128


def lookup(table, index):
    row = lax.broadcasted_iota(jnp.int32, (8, 128), 0)
    lane = jnp.bitwise_and(index, 127)
    part = jnp.right_shift(index, 7)
    out = jnp.zeros_like(table)
    for k in range(4):
        low = jnp.broadcast_to(table[k : k + 1], (8, 128))
        high = jnp.broadcast_to(table[4 + k : 5 + k], (8, 128))
        spread = jnp.where(row < 4, low, high)
        found = jnp.take_along_axis(spread, lane, axis=1, mode="promise_in_bounds")
        out = jnp.where(part == k, found, out)
    return out


def picker(index, count):
    rows = lax.broadcasted_iota(jnp.int32, (count, 128), 0)
    return jnp.where(rows == index, 1.0, 0.0).astype(BF)


def dot(a, b):
    return jnp.dot(a, b, preferred_element_type=jnp.float32)


def dot_t(a, b):
    return lax.dot_general(a, b, (((1,), (1,)), ((), ())), preferred_element_type=jnp.float32)


def lanes(parts):
    return jnp.concatenate(parts, axis=1)


def inverse(kept, values):
    row = lax.broadcasted_iota(jnp.int32, (16, 128), 0)
    total = jnp.zeros((16, 640), jnp.float32)
    for k in range(4):
        value = values[k : k + 1] + 1
        high = jnp.broadcast_to(jnp.right_shift(value, 6), (16, 128))
        low = jnp.broadcast_to(jnp.bitwise_and(value, 63), (16, 128))
        digits = jnp.where(row == 0, high, jnp.where(row == 1, low, 0)).astype(jnp.float32).astype(BF)
        total = total + dot_t(digits, picker(kept[k : k + 1], 640))
    return (total[0:1] * 64.0 + total[1:2]).astype(jnp.int32) - 1


def half(rows, which):
    return jnp.where(which == 0, rows[0:4], rows[4:8])


def kernel(offs, kv, q, keep, goal, attn, mass, owned, recv, spans, keeps, own, owns, marks, cz, late, cache, valid, tab, metas, tabl, obuf,
           s_sp, s_ke, s_ow, s_ma, s_cz, r_sp, r_ke, r_ow, r_ma, r_cz, s_la, r_la,
           s_up, r_up, s_dn, r_dn, s_mu, r_mu, s_md, r_md, s_lu, r_lu, s_ld, r_ld, s_ex, r_ex, s_lo):
    j = lax.axis_index("ctx")
    x = lax.axis_index("kv")
    z = j // 8
    i = lax.rem(j, 8)
    y = i // 2
    c = lax.rem(i, 2)
    me = i * 4 + x
    early = jnp.where(offs[0] == 0, 0, 1)

    def zdev(n):
        return (n * 8 + i, x)

    def pdev(n):
        return (z * 8 + n, x)

    def mdev(n):
        return (z * 8 + n // 4, lax.rem(n, 4))

    barrier = pltpu.get_barrier_semaphore()

    @pl.loop(1, 32)
    def _(k):
        pl.semaphore_signal(barrier, inc=1, device_id=mdev(lax.rem(me + k, 32)), device_id_type=MESH)

    @pl.loop(1, 8)
    def _(k):
        pl.semaphore_signal(barrier, inc=1, device_id=zdev(lax.rem(z + k, 8)), device_id_type=MESH)

    for p in range(2):
        lists = keep[early if p == 0 else 1 - early]
        for h in range(2):
            for k in range(4):
                at = p * 8 + h * 4 + k
                keeps[i, at : at + 1, :] = lists[h : h + 1, k * 128 : (k + 1) * 128]
    keeps[i, 16:20, :] = goal[early]
    keeps[i, 20:24, :] = goal[1 - early]
    for b in range(4):
        spans[i, b * 128 : (b + 1) * 128, :] = kv[early, :, b].reshape(128, 128).T
    final_pair = j >= 62

    @pl.when(final_pair)
    def _():
        for b in range(4):
            late[c, b * 128 : (b + 1) * 128, :] = kv[1 - early, :, b].reshape(128, 128).T

    pl.semaphore_wait(barrier, 38)

    def send(src, dst, ss, rs, dev):
        return pltpu.make_async_remote_copy(
            src_ref=src, dst_ref=dst, send_sem=ss, recv_sem=rs, device_id=dev, device_id_type=MESH
        )

    def took(view, sem):
        pltpu.make_async_copy(view, view, sem).wait()

    def arrive(buf, sem, k):
        took(buf.at[k], sem.at[k])

    def late_copy():
        return send(late.at[c], late.at[c], s_la, r_la, pdev(7 - c))

    waits = []
    for k in range(1, 8):
        copy = send(keeps.at[i], keeps.at[i], s_ke.at[k], r_ke.at[i], pdev(lax.rem(i + k, 8)))
        copy.start()
        waits.append(copy)
    for k in range(1, 8):
        copy = send(spans.at[i], spans.at[i], s_sp.at[k], r_sp.at[i], pdev(lax.rem(i + k, 8)))
        copy.start()
        waits.append(copy)

    @pl.when(final_pair)
    def _():
        late_copy().start()

    for k in range(1, 8):
        arrive(keeps, r_ke, lax.rem(i + k, 8))
    slot = lax.rem(lax.broadcasted_iota(jnp.int32, (8, 128), 0), 4) * 128 + lax.broadcasted_iota(jnp.int32, (8, 128), 1)
    pre, mine = slot, slot
    for n in range(8):
        mine = jnp.where(i == n, pre, mine)
        kept = keeps[n, 0:8, :]
        pre = jnp.where(kept < 512, lookup(pre, jnp.minimum(kept, 511)), kept + 128 * n)
    marks[z] = pre

    def marks_copy(k):
        return send(marks.at[z], marks.at[z], s_ma.at[k], r_ma.at[z], zdev(z + k))

    def own_copy(k):
        return send(own, owns.at[z], s_ow.at[k], r_ow.at[z], zdev(z + k))

    for k in range(1, 8):
        @pl.when(z + k < 8)
        def _():
            marks_copy(k).start()

    first, second = i - c, i - c + 1
    goal0 = keeps[first, 16:20, :]
    goal1 = inverse(half(keeps[second, 0:8, :], c), keeps[second, 16:20, :])
    metas[z, 0:4, :] = goal0
    metas[z, 4:8, :] = jnp.full((4, 128), -1, jnp.int32)
    for k in range(5):
        metas[z, 8 + k : 9 + k, :] = goal1[:, k * 128 : (k + 1) * 128]
    metas[z, 13:16, :] = jnp.full((3, 128), -1, jnp.int32)

    @pl.when(final_pair)
    def _():
        kept0 = half(keeps[first, 8:16, :], c)
        kept1 = half(keeps[second, 8:16, :], c)
        out1 = inverse(kept1, keeps[second, 20:24, :])
        back = jnp.concatenate([out1[:, k * 128 : (k + 1) * 128] for k in range(4)], axis=0)
        metas[z, 5:6, :] = inverse(kept0, keeps[first, 20:24, :])[:, 512:640]
        metas[z, 13:14, :] = inverse(kept0, back)[:, 512:640]
        metas[z, 14:15, :] = out1[:, 512:640]

    for k in range(1, 8):
        arrive(spans, r_sp, lax.rem(i + k, 8))
    cols = pl.ds(pl.multiple_of(i * 64, 64), 64)
    head = jnp.where(i < 4, pre[0:4], pre[4:8])
    unit = lanes([spans[n, cols, :] for n in range(8)])
    for k in range(4):
        own[k * 64 : (k + 1) * 64, :] = dot(unit, picker(head[k : k + 1] - 512, 1024)).astype(BF)
    for k in range(1, 8):
        @pl.when(z + k < 8)
        def _():
            own_copy(k).start()

    for h in range(2):
        table = lanes([spans[n, h * 256 : (h + 1) * 256, :] for n in range(8)])
        for k in range(4):
            cache[0, k, h * 256 : (h + 1) * 256, :] = dot(table, picker(mine[h * 4 + k : h * 4 + k + 1] - 512, 1024)).astype(BF)

    for n in range(7):
        @pl.when(n < z)
        def _():
            arrive(marks, r_ma, n)
    cur = jnp.full((8, 128), -1, jnp.int32)
    for n in range(7):
        m = jnp.where(n < z, marks[n], slot)
        new = jnp.where(m < 512, lookup(cur, jnp.minimum(m, 511)), n * 512 + slot)
        cur = jnp.where(n < z, new, cur)
    chead = jnp.where(i < 4, cur[0:4], cur[4:8])
    part = cz.at[i]
    part[...] = jnp.zeros((256, 128), BF)
    for n in range(7):
        @pl.when(n < z)
        def _():
            arrive(owns, r_ow, n)
            table = lanes([owns[n, p * 64 : (p + 1) * 64, :] for p in range(4)])
            for k in range(4):
                part[k * 64 : (k + 1) * 64, :] += dot(table, picker(chead[k : k + 1] - n * 512, 512)).astype(BF)
    for k in range(1, 8):
        copy = send(cz.at[i], cz.at[i], s_cz.at[k], r_cz.at[i], pdev(lax.rem(i + k, 8)))
        copy.start()
        waits.append(copy)
    was = jnp.where(cur >= 0, 1, 0)
    valid[0] = jnp.where(mine >= 512, 1, lookup(was, jnp.minimum(mine, 511)))

    @pl.when(final_pair)
    def _():
        took(late.at[1 - c], r_la)
        for h in range(2):
            tabl[h] = late[h, pl.ds(pl.multiple_of(c * 256, 256), 256), :]

    for k in range(1, 8):
        arrive(cz, r_cz, lax.rem(i + k, 8))
    for h in range(2):
        table = jnp.concatenate(
            [lanes([cz[n, p * 64 : (p + 1) * 64, :] for p in range(4)]) for n in range(h * 4, h * 4 + 4)], axis=0
        )
        for k in range(4):
            cache[0, k, h * 256 : (h + 1) * 256, :] += dot(table, picker(mine[h * 4 + k : h * 4 + k + 1], 512)).astype(BF)

    tab[z, 4] = spans[second, pl.ds(pl.multiple_of(c * 256, 256), 256), :]

    @pl.when(c == 1)
    def _():
        for k in range(4):
            tab[z, k] = cache[0, k, 256:512, :]

    @pl.when(c == 0)
    def _():
        table = lanes([cache[0, k, 0:256, :] for k in range(4)] + [spans[i, 0:256, :]])
        kept = keeps[i, 0:8, :]
        for k in range(4):
            tab[z, k] = dot(table, picker(kept[k : k + 1], 640)).astype(BF)

    above, below = zdev(lax.rem(z + 1, 8)), zdev(lax.rem(z + 7, 8))

    WAYS = (("up", 1), ("down", -1))

    def chunks(way, s):
        return range(5) if s < 4 else (range(2) if way == "up" else range(2, 5))

    def origin(way, s):
        return lax.rem(z + 8 - s, 8) if way == "up" else lax.rem(z + s, 8)

    def chunk_copy(way, s, k):
        o = origin(way, s - 1)
        ss, rs, to = (s_up, r_up, above) if way == "up" else (s_dn, r_dn, below)
        return send(tab.at[o, k], tab.at[o, k], ss.at[s * 5 + k], rs.at[s * 5 + k], to)

    def metas_copy(way, s):
        o = origin(way, s - 1)
        ss, rs, to = (s_mu, r_mu, above) if way == "up" else (s_md, r_md, below)
        return send(metas.at[o], metas.at[o], ss.at[s], rs.at[s], to)

    def tabl_copy(way):
        ss, rs, to = (s_lu, r_lu, above) if way == "up" else (s_ld, r_ld, below)
        return send(tabl, tabl, ss, rs, to)

    def has_late(way, s):
        return (origin(way, s) == 7) & (y == 3)

    def goes(way, s):
        return s <= (4 if way == "up" else 3)

    def lead(s):
        for way, _ in WAYS:
            if goes(way, s):
                metas_copy(way, s).start()

                @pl.when(has_late(way, s - 1))
                def _():
                    tabl_copy(way).start()

    def receive(s, tasks):
        for way, _ in WAYS:
            if goes(way, s):
                took(metas.at[origin(way, s)], (r_mu if way == "up" else r_md).at[s])

                @pl.when(has_late(way, s))
                def _():
                    took(tabl, r_lu if way == "up" else r_ld)
        if s < 4:
            lead(s + 1)
        for k in range(5):
            for way, _ in WAYS:
                if k in chunks(way, s):
                    took(tab.at[origin(way, s), k], (r_up if way == "up" else r_dn).at[s * 5 + k])
                if s < 4 and k in chunks(way, s + 1):
                    chunk_copy(way, s + 1, k).start()
            if k < len(tasks):
                tasks[k]()

    def passed(s):
        for way, _ in WAYS:
            for k in chunks(way, s):
                chunk_copy(way, s, k).wait_send()
            if goes(way, s):
                metas_copy(way, s).wait_send()

                @pl.when(has_late(way, s - 1))
                def _():
                    tabl_copy(way).wait_send()

    def exchange(o, n):
        dst = recv.at[pl.ds(x * 4 + c * 2, 2), pl.ds(pl.multiple_of((o * 4 + y) * 16, 16), 16), :]
        return send(obuf.at[o, :, pl.ds(pl.multiple_of(n * 16, 16), 16), :], dst, s_ex.at[o], r_ex.at[o], mdev(n))

    def keep_local(o):
        dst = recv.at[pl.ds(x * 4 + c * 2, 2), pl.ds(pl.multiple_of((o * 4 + y) * 16, 16), 16), :]
        return pltpu.make_async_copy(obuf.at[o, :, pl.ds(pl.multiple_of(me * 16, 16), 16), :], dst, s_lo.at[o])

    line = lax.broadcasted_iota(jnp.int32, (512, 128), 0)
    place = z * 256 + jnp.right_shift(line, 4) * 8 + jnp.bitwise_and(line, 7)
    later = jnp.bitwise_and(line, 8) > 0

    def hit(o, k):
        wanted = jnp.where(later, metas[o, 8 + k : 9 + k, :], metas[o, k : k + 1, :])
        return jnp.where(wanted == place, 1.0, 0.0).astype(BF)

    def hand_out(o):
        rows = dot_t(lanes([hit(o, k) for k in range(5)]), lanes([tab[o, k] for k in range(5)])).astype(BF)
        obuf[o, 0] = rows[:, 0:128]
        obuf[o, 1] = rows[:, 128:256]

        @pl.when((o == 7) & (y == 3))
        def _():
            rows = dot_t(lanes([hit(o, k) for k in (5, 6)]), lanes([tabl[k] for k in range(2)])).astype(BF)
            obuf[o, 0] += rows[:, 0:128]
            obuf[o, 1] += rows[:, 128:256]

        @pl.loop(1, 32)
        def _(k):
            exchange(o, lax.rem(me + k, 32)).start()

        keep_local(o).start()

    own_tokens = lax.broadcasted_iota(jnp.int32, (128, 128), 1) <= lax.broadcasted_iota(jnp.int32, (128, 128), 0)

    def attend(p, h, span_t):
        def chunk(at):
            return lanes([cache[p, k, at : at + 128, :] for k in range(4)] + [span_t[at : at + 128, :]])

        keys, values = chunk(h * 256), chunk(h * 256 + 128)
        seen = lanes([jnp.broadcast_to(valid[p, h * 4 + k : h * 4 + k + 1, :], (128, 128)) for k in range(4)]) > 0
        near = own_tokens
        prompt = early if p == 0 else 1 - early
        scale = 1.0 / math.sqrt(HEAD)

        def one(g, total):
            scores = dot(q[prompt, :, h * 8 + g].reshape(128, 128), keys) * scale
            old = jnp.where(seen, scores[:, 0:512], -1e30)
            new = jnp.where(near, scores[:, 512:640], -1e30)
            peak = jnp.maximum(jnp.max(old, axis=1, keepdims=True), jnp.max(new, axis=1, keepdims=True))
            expo = lanes([jnp.where(seen, jnp.exp(old - peak), 0.0), jnp.where(near, jnp.exp(new - peak), 0.0)])
            weights = expo * (1.0 / jnp.sum(expo, axis=1, keepdims=True))
            mixed = dot_t(weights.astype(BF), values)
            at = pl.ds(pl.multiple_of((h * 8 + g) * 128, 128), 128)
            for n in range(2):
                part = jnp.where(prompt == n, mixed, 0.0)
                if p == 1:
                    part = part + attn[n, :, at].astype(jnp.float32)
                attn[n, :, at] = part.astype(BF)
            return total + jnp.sum(weights.reshape(16, 8, 640), axis=0)

        total = lax.fori_loop(0, 8, one, jnp.zeros((8, 640), jnp.float32))
        total = jnp.sum(total, axis=0, keepdims=True)
        for n in range(2):
            part = jnp.where(prompt == n, total, 0.0)
            mass[n, h : h + 1, :] = part + mass[n, h : h + 1, :] if p == 1 else part

    def attend_late():
        @pl.when(final_pair)
        def _():
            cache[1] = jnp.zeros((4, 512, 128), BF)
            valid[1] = jnp.zeros((8, 128), jnp.int32)

            @pl.when(c == 1)
            def _():
                kept = keeps[first, 8:16, :]
                valid[1] = jnp.where(kept >= 512, 1, 0)
                for h in range(2):
                    for k in range(4):
                        cache[1, k, h * 256 : (h + 1) * 256, :] = dot(
                            late[0, h * 256 : (h + 1) * 256, :], picker(kept[h * 4 + k : h * 4 + k + 1] - 512, 128)
                        ).astype(BF)

            for h in range(2):
                attend(1, h, late.at[c])

    lead(1)
    for k in range(5):
        for way, _ in WAYS:
            chunk_copy(way, 1, k).start()

    def hand(way, s):
        return lambda: hand_out(origin(way, s))

    hand_out(z)
    receive(1, [lambda: attend(0, 0, spans.at[i])])
    receive(2, [hand("up", 1), hand("down", 1), lambda: attend(0, 1, spans.at[i])])
    receive(3, [hand("up", 2), hand("down", 2), attend_late])
    receive(4, [hand("up", 3), hand("down", 3)])
    hand_out(origin("up", 4))

    for copy in waits:
        copy.wait_send()
    for k in range(1, 8):
        @pl.when(z + k < 8)
        def _():
            marks_copy(k).wait_send()
            own_copy(k).wait_send()

    @pl.when(final_pair)
    def _():
        late_copy().wait_send()

    for s in (1, 2, 3, 4):
        passed(s)

    for s, way in ((0, "up"), (1, "up"), (1, "down"), (2, "up"), (2, "down"), (3, "up"), (3, "down"), (4, "up")):
        o = origin(way, s)
        keep_local(o).wait()
        took(obuf.at[o, :, pl.ds(0, 496), :], s_ex.at[o])
        took(recv.at[pl.ds(0, 2), pl.ds(0, 496), :], r_ex.at[o])
        rows = pl.ds(pl.multiple_of(o * 64, 64), 64)
        for b in range(16):
            owned[rows, b * 128 : (b + 1) * 128] = recv[b, rows, :]


def whole(offsets, kv, q, keep, goal):
    V, D = pltpu.VMEM, pltpu.SemaphoreType.DMA
    vmem = pl.BlockSpec(memory_space=V)
    return pl.pallas_call(
        kernel,
        out_shape=(
            jax.ShapeDtypeStruct((2, 128, 2048), BF),
            jax.ShapeDtypeStruct((2, 2, 640), jnp.float32),
            jax.ShapeDtypeStruct((512, 2048), BF),
        ),
        in_specs=[pl.BlockSpec(memory_space=pltpu.SMEM)] + [vmem] * 4,
        out_specs=(vmem,) * 3,
        scratch_shapes=[
            V((16, 512, 128), BF),
            V((8, 512, 128), BF),
            V((8, 24, 128), jnp.int32),
            V((256, 128), BF),
            V((8, 256, 128), BF),
            V((8, 8, 128), jnp.int32),
            V((8, 256, 128), BF),
            V((2, 512, 128), BF),
            V((2, 4, 512, 128), BF),
            V((2, 8, 128), jnp.int32),
            V((8, 5, 256, 128), BF),
            V((8, 16, 128), jnp.int32),
            V((2, 256, 128), BF),
            V((8, 2, 512, 128), BF),
        ]
        + [D((8,))] * 10
        + [D] * 2
        + [D((25,))] * 4
        + [D((5,))] * 4
        + [D] * 4
        + [D((8,))] * 3,
        compiler_params=pltpu.CompilerParams(collective_id=0, has_side_effects=True, vmem_limit_bytes=40 << 20),
    )(offsets, kv, q, keep, goal)


def placed_rows(owner_ids, capacity):
    count = owner_ids.shape[0]
    before = jnp.arange(count)[None, :] < jnp.arange(count)[:, None]
    same = owner_ids[None, :] == owner_ids[:, None]
    rank = jnp.sum(jnp.where(before & same, 1, 0), axis=1)
    return owner_ids * capacity + rank


def tiled(rows):
    prompts, count, width = rows.shape
    return jnp.transpose(rows.reshape(prompts, count // 8, 8, width // 128, 128), (0, 1, 3, 2, 4))


def local(query, kv_rows, keep, dest, offsets):
    return whole(
        offsets,
        tiled(kv_rows),
        tiled(query),
        keep[:, 0],
        placed_rows(dest[:, 0], 8).reshape(2, 4, 128),
    )


def solution(mesh):
    placed = (
        P(None, "ctx", "kv"),
        P(None, "ctx", "kv"),
        P(None, "ctx", "kv", None),
        P("ctx", None),
        P(),
    )
    return jax.shard_map(
        local,
        mesh=mesh,
        in_specs=placed,
        out_specs=(P(None, "ctx", "kv"), P(None, "kv", "ctx"), P(("ctx", "kv"), None)),
        check_vma=False,
    )
```

```python
import math

import jax
import jax.numpy as jnp
from jax import lax
from jax.experimental import pallas as pl
from jax.experimental.pallas import tpu as pltpu
from jax.sharding import PartitionSpec as P

MESH = pl.DeviceIdType.MESH
BF = jnp.bfloat16
HEAD = 128


def lookup(table, index):
    row = lax.broadcasted_iota(jnp.int32, (8, 128), 0)
    lane = jnp.bitwise_and(index, 127)
    part = jnp.right_shift(index, 7)
    out = jnp.zeros_like(table)
    for k in range(4):
        low = jnp.broadcast_to(table[k : k + 1], (8, 128))
        high = jnp.broadcast_to(table[4 + k : 5 + k], (8, 128))
        spread = jnp.where(row < 4, low, high)
        found = jnp.take_along_axis(spread, lane, axis=1, mode="promise_in_bounds")
        out = jnp.where(part == k, found, out)
    return out


def picker(index, count):
    rows = lax.broadcasted_iota(jnp.int32, (count, 128), 0)
    return jnp.where(rows == index, 1.0, 0.0).astype(BF)


def dot(a, b):
    return jnp.dot(a, b, preferred_element_type=jnp.float32)


def dot_t(a, b):
    return lax.dot_general(a, b, (((1,), (1,)), ((), ())), preferred_element_type=jnp.float32)


def lanes(parts):
    return jnp.concatenate(parts, axis=1)


def inverse(kept, values):
    row = lax.broadcasted_iota(jnp.int32, (16, 128), 0)
    total = jnp.zeros((16, 640), jnp.float32)
    for k in range(4):
        value = values[k : k + 1] + 1
        high = jnp.broadcast_to(jnp.right_shift(value, 6), (16, 128))
        low = jnp.broadcast_to(jnp.bitwise_and(value, 63), (16, 128))
        digits = jnp.where(row == 0, high, jnp.where(row == 1, low, 0)).astype(jnp.float32).astype(BF)
        total = total + dot_t(digits, picker(kept[k : k + 1], 640))
    return (total[0:1] * 64.0 + total[1:2]).astype(jnp.int32) - 1


def half(rows, which):
    return jnp.where(which == 0, rows[0:4], rows[4:8])


def kernel(offs, kv, q, keep, dest, attn, mass, owned, recv, spans, keeps, units, goals, own, owns, marks, cz, late, cache, valid, tab, metas, tabl, obuf,
           s_sp, s_ke, s_ow, s_ma, s_cz, r_sp, r_ke, r_ow, r_ma, r_cz, s_la, r_la,
           s_up, r_up, s_dn, r_dn, s_lu, r_lu, s_ld, r_ld, s_ex, r_ex, s_lo, s_un, r_un, s_me, r_me, r_c4, s_c4, s_go, r_go):
    j = lax.axis_index("ctx")
    x = lax.axis_index("kv")
    z = j // 8
    i = lax.rem(j, 8)
    y = i // 2
    c = lax.rem(i, 2)
    me = i * 4 + x
    early = jnp.where(offs[0] == 0, 0, 1)

    def zdev(n):
        return (n * 8 + i, x)

    def pdev(n):
        return (z * 8 + n, x)

    def pair(n, core):
        return (n * 8 + y * 2 + core, x)

    def mdev(n):
        return (z * 8 + n // 4, lax.rem(n, 4))

    barrier = pltpu.get_barrier_semaphore()

    @pl.loop(1, 32)
    def _(k):
        pl.semaphore_signal(barrier, inc=1, device_id=mdev(lax.rem(me + k, 32)), device_id_type=MESH)

    @pl.loop(1, 8)
    def _(k):
        for n in range(2):
            pl.semaphore_signal(barrier, inc=1, device_id=pair(lax.rem(z + k, 8), n), device_id_type=MESH)

    for p in range(2):
        lists = keep[early if p == 0 else 1 - early]
        for h in range(2):
            for k in range(4):
                at = p * 8 + h * 4 + k
                keeps[i, at : at + 1, :] = lists[h : h + 1, k * 128 : (k + 1) * 128]
    for b in range(4):
        spans[i, b * 128 : (b + 1) * 128, :] = kv[early, :, b].reshape(128, 128).T
    final_pair = j >= 62

    @pl.when(final_pair)
    def _():
        for b in range(4):
            late[c, b * 128 : (b + 1) * 128, :] = kv[1 - early, :, b].reshape(128, 128).T

    cols = pl.ds(pl.multiple_of(i * 64, 64), 64)
    units[i] = spans[i, cols, :]
    pl.semaphore_wait(barrier, 45)

    def send(src, dst, ss, rs, dev):
        return pltpu.make_async_remote_copy(
            src_ref=src, dst_ref=dst, send_sem=ss, recv_sem=rs, device_id=dev, device_id_type=MESH
        )

    def took(view, sem):
        pltpu.make_async_copy(view, view, sem).wait()

    def arrive(buf, sem, k):
        took(buf.at[k], sem.at[k])

    def late_copy():
        return send(late.at[c], late.at[c], s_la, r_la, pdev(7 - c))

    waits = []
    for k in range(1, 8):
        copy = send(keeps.at[i], keeps.at[i], s_ke.at[k], r_ke.at[i], pdev(lax.rem(i + k, 8)))
        copy.start()
        waits.append(copy)
    for k in range(1, 8):
        n = lax.rem(i + k, 8)
        copy = send(spans.at[i, pl.ds(pl.multiple_of(n * 64, 64), 64), :], units.at[i], s_un.at[k], r_un.at[i], pdev(n))
        copy.start()
        waits.append(copy)
    for k in range(1, 8):
        copy = send(spans.at[i], spans.at[i], s_sp.at[k], r_sp.at[i], pdev(lax.rem(i + k, 8)))
        copy.start()
        waits.append(copy)

    @pl.when(final_pair)
    def _():
        late_copy().start()

    for k in range(1, 8):
        arrive(keeps, r_ke, lax.rem(i + k, 8))
    slot = lax.rem(lax.broadcasted_iota(jnp.int32, (8, 128), 0), 4) * 128 + lax.broadcasted_iota(jnp.int32, (8, 128), 1)
    pre, mine = slot, slot
    for n in range(8):
        mine = jnp.where(i == n, pre, mine)
        kept = keeps[n, 0:8, :]
        pre = jnp.where(kept < 512, lookup(pre, jnp.minimum(kept, 511)), kept + 128 * n)
    marks[z] = pre

    def marks_copy(k):
        return send(marks.at[z], marks.at[z], s_ma.at[k], r_ma.at[z], zdev(z + k))

    def own_copy(k):
        return send(own, owns.at[z], s_ow.at[k], r_ow.at[z], zdev(z + k))

    for k in range(1, 8):
        @pl.when(z + k < 8)
        def _():
            marks_copy(k).start()

    for k in range(1, 8):
        arrive(units, r_un, lax.rem(i + k, 8))
    head = jnp.where(i < 4, pre[0:4], pre[4:8])
    unit = lanes([units[n] for n in range(8)])
    for k in range(4):
        own[k * 64 : (k + 1) * 64, :] = dot(unit, picker(head[k : k + 1] - 512, 1024)).astype(BF)
    for k in range(1, 8):
        @pl.when(z + k < 8)
        def _():
            own_copy(k).start()

    owners = dest[...]
    side = lax.broadcasted_iota(jnp.int32, (128, 128), 0) < lax.broadcasted_iota(jnp.int32, (128, 128), 1)
    earlier = jnp.where(side, 1.0, 0.0).astype(BF)
    count = jnp.zeros((256, 1), jnp.float32)
    for n in range(8):
        named = picker(owners[n : n + 1], 256)
        before = dot(named, earlier) + count
        named = named.astype(jnp.float32)
        rank = jnp.sum(named * before, axis=0, keepdims=True)
        count = count + jnp.sum(named, axis=1, keepdims=True)
        goals[c, n : n + 1, :] = owners[n : n + 1] * 8 + rank.astype(jnp.int32)
    first, second = i - c, i - c + 1
    copy = send(goals.at[c], goals.at[c], s_go, r_go, pdev(first + 1 - c))
    copy.start()
    waits.append(copy)

    for k in range(1, 8):
        arrive(spans, r_sp, lax.rem(i + k, 8))
    for h in range(2):
        table = lanes([spans[n, h * 256 : (h + 1) * 256, :] for n in range(8)])
        for k in range(4):
            cache[0, k, h * 256 : (h + 1) * 256, :] = dot(table, picker(mine[h * 4 + k : h * 4 + k + 1] - 512, 1024)).astype(BF)

    took(goals.at[1 - c], r_go)
    goal0 = half(goals[0], early)
    goal1 = inverse(half(keeps[second, 0:8, :], c), half(goals[1], early))
    metas[z, 0:4, :] = goal0
    metas[z, 4:8, :] = jnp.full((4, 128), -1, jnp.int32)
    for k in range(5):
        metas[z, 8 + k : 9 + k, :] = goal1[:, k * 128 : (k + 1) * 128]
    metas[z, 13:16, :] = jnp.full((3, 128), -1, jnp.int32)

    @pl.when(final_pair)
    def _():
        kept0 = half(keeps[first, 8:16, :], c)
        kept1 = half(keeps[second, 8:16, :], c)
        out1 = inverse(kept1, half(goals[1], 1 - early))
        back = jnp.concatenate([out1[:, k * 128 : (k + 1) * 128] for k in range(4)], axis=0)
        metas[z, 5:6, :] = inverse(kept0, half(goals[0], 1 - early))[:, 512:640]
        metas[z, 13:14, :] = inverse(kept0, back)[:, 512:640]
        metas[z, 14:15, :] = out1[:, 512:640]

    for k in range(1, 8):
        copy = send(metas.at[z], metas.at[z], s_me.at[k], r_me.at[z], zdev(lax.rem(z + k, 8)))
        copy.start()
        waits.append(copy)

    for n in range(7):
        @pl.when(n < z)
        def _():
            arrive(marks, r_ma, n)
    cur = jnp.full((8, 128), -1, jnp.int32)
    for n in range(7):
        m = jnp.where(n < z, marks[n], slot)
        new = jnp.where(m < 512, lookup(cur, jnp.minimum(m, 511)), n * 512 + slot)
        cur = jnp.where(n < z, new, cur)
    chead = jnp.where(i < 4, cur[0:4], cur[4:8])
    part = cz.at[i]
    part[...] = jnp.zeros((256, 128), BF)
    for n in range(7):
        @pl.when(n < z)
        def _():
            arrive(owns, r_ow, n)
            table = lanes([owns[n, p * 64 : (p + 1) * 64, :] for p in range(4)])
            for k in range(4):
                part[k * 64 : (k + 1) * 64, :] += dot(table, picker(chead[k : k + 1] - n * 512, 512)).astype(BF)
    for k in range(1, 8):
        copy = send(cz.at[i], cz.at[i], s_cz.at[k], r_cz.at[i], pdev(lax.rem(i + k, 8)))
        copy.start()
        waits.append(copy)

    def span_copies():
        return [
            send(spans.at[i, n * 256 : (n + 1) * 256, :], tab.at[z, 4], s_c4.at[k * 2 + n], r_c4.at[z], pair(lax.rem(z + k, 8), n))
            for k in range(1, 8)
            for n in range(2)
        ]

    @pl.when(c == 1)
    def _():
        for copy in span_copies():
            copy.start()

    was = jnp.where(cur >= 0, 1, 0)
    valid[0] = jnp.where(mine >= 512, 1, lookup(was, jnp.minimum(mine, 511)))

    @pl.when(final_pair)
    def _():
        took(late.at[1 - c], r_la)
        for h in range(2):
            tabl[h] = late[h, pl.ds(pl.multiple_of(c * 256, 256), 256), :]

    for k in range(1, 8):
        arrive(cz, r_cz, lax.rem(i + k, 8))
    for h in range(2):
        table = jnp.concatenate(
            [lanes([cz[n, p * 64 : (p + 1) * 64, :] for p in range(4)]) for n in range(h * 4, h * 4 + 4)], axis=0
        )
        for k in range(4):
            cache[0, k, h * 256 : (h + 1) * 256, :] += dot(table, picker(mine[h * 4 + k : h * 4 + k + 1], 512)).astype(BF)

    tab[z, 4] = spans[second, pl.ds(pl.multiple_of(c * 256, 256), 256), :]

    @pl.when(c == 1)
    def _():
        for k in range(4):
            tab[z, k] = cache[0, k, 256:512, :]

    @pl.when(c == 0)
    def _():
        table = lanes([cache[0, k, 0:256, :] for k in range(4)] + [spans[i, 0:256, :]])
        kept = keeps[i, 0:8, :]
        for k in range(4):
            tab[z, k] = dot(table, picker(kept[k : k + 1], 640)).astype(BF)

    above, below = zdev(lax.rem(z + 1, 8)), zdev(lax.rem(z + 7, 8))

    WAYS = (("up", 1), ("down", -1))

    def chunks(way, s):
        return range(4) if s < 4 else (range(2) if way == "up" else range(2, 4))

    def origin(way, s):
        return lax.rem(z + 8 - s, 8) if way == "up" else lax.rem(z + s, 8)

    def chunk_copy(way, s, k):
        o = origin(way, s - 1)
        ss, rs, to = (s_up, r_up, above) if way == "up" else (s_dn, r_dn, below)
        return send(tab.at[o, k], tab.at[o, k], ss.at[s * 5 + k], rs.at[s * 5 + k], to)

    def tabl_copy(way):
        ss, rs, to = (s_lu, r_lu, above) if way == "up" else (s_ld, r_ld, below)
        return send(tabl, tabl, ss, rs, to)

    def has_late(way, s):
        return (origin(way, s) == 7) & (y == 3)

    def goes(way, s):
        return s <= (4 if way == "up" else 3)

    def lead(s):
        for way, _ in WAYS:
            if goes(way, s):
                @pl.when(has_late(way, s - 1))
                def _():
                    tabl_copy(way).start()

    def receive(s, tasks):
        for way, _ in WAYS:
            if goes(way, s):
                @pl.when(has_late(way, s))
                def _():
                    took(tabl, r_lu if way == "up" else r_ld)
        if s < 4:
            lead(s + 1)
        for k in range(4):
            for way, _ in WAYS:
                if k in chunks(way, s):
                    took(tab.at[origin(way, s), k], (r_up if way == "up" else r_dn).at[s * 5 + k])
                if s < 4 and k in chunks(way, s + 1):
                    chunk_copy(way, s + 1, k).start()
            if k < len(tasks):
                tasks[k]()

    def passed(s):
        for way, _ in WAYS:
            for k in chunks(way, s):
                chunk_copy(way, s, k).wait_send()
            if goes(way, s):
                @pl.when(has_late(way, s - 1))
                def _():
                    tabl_copy(way).wait_send()

    def exchange(o, n):
        dst = recv.at[pl.ds(x * 4 + c * 2, 2), pl.ds(pl.multiple_of((o * 4 + y) * 16, 16), 16), :]
        return send(obuf.at[o, :, pl.ds(pl.multiple_of(n * 16, 16), 16), :], dst, s_ex.at[o], r_ex.at[o], mdev(n))

    def keep_local(o):
        dst = recv.at[pl.ds(x * 4 + c * 2, 2), pl.ds(pl.multiple_of((o * 4 + y) * 16, 16), 16), :]
        return pltpu.make_async_copy(obuf.at[o, :, pl.ds(pl.multiple_of(me * 16, 16), 16), :], dst, s_lo.at[o])

    line = lax.broadcasted_iota(jnp.int32, (512, 128), 0)
    place = z * 256 + jnp.right_shift(line, 4) * 8 + jnp.bitwise_and(line, 7)
    later = jnp.bitwise_and(line, 8) > 0

    def hit(o, k):
        wanted = jnp.where(later, metas[o, 8 + k : 9 + k, :], metas[o, k : k + 1, :])
        return jnp.where(wanted == place, 1.0, 0.0).astype(BF)

    def hand_out(o):
        rows = dot_t(lanes([hit(o, k) for k in range(5)]), lanes([tab[o, k] for k in range(5)])).astype(BF)
        obuf[o, 0] = rows[:, 0:128]
        obuf[o, 1] = rows[:, 128:256]

        @pl.when((o == 7) & (y == 3))
        def _():
            rows = dot_t(lanes([hit(o, k) for k in (5, 6)]), lanes([tabl[k] for k in range(2)])).astype(BF)
            obuf[o, 0] += rows[:, 0:128]
            obuf[o, 1] += rows[:, 128:256]

        @pl.loop(1, 32)
        def _(k):
            exchange(o, lax.rem(me + k, 32)).start()

        keep_local(o).start()

    own_tokens = lax.broadcasted_iota(jnp.int32, (128, 128), 1) <= lax.broadcasted_iota(jnp.int32, (128, 128), 0)

    def attend(p, h, span_t):
        def chunk(at):
            return lanes([cache[p, k, at : at + 128, :] for k in range(4)] + [span_t[at : at + 128, :]])

        keys, values = chunk(h * 256), chunk(h * 256 + 128)
        seen = lanes([jnp.broadcast_to(valid[p, h * 4 + k : h * 4 + k + 1, :], (128, 128)) for k in range(4)]) > 0
        near = own_tokens
        prompt = early if p == 0 else 1 - early
        scale = 1.0 / math.sqrt(HEAD)

        def one(g, total):
            scores = dot(q[prompt, :, h * 8 + g].reshape(128, 128), keys) * scale
            old = jnp.where(seen, scores[:, 0:512], -1e30)
            new = jnp.where(near, scores[:, 512:640], -1e30)
            peak = jnp.maximum(jnp.max(old, axis=1, keepdims=True), jnp.max(new, axis=1, keepdims=True))
            expo = lanes([jnp.where(seen, jnp.exp(old - peak), 0.0), jnp.where(near, jnp.exp(new - peak), 0.0)])
            weights = expo * (1.0 / jnp.sum(expo, axis=1, keepdims=True))
            mixed = dot_t(weights.astype(BF), values)
            at = pl.ds(pl.multiple_of((h * 8 + g) * 128, 128), 128)
            for n in range(2):
                part = jnp.where(prompt == n, mixed, 0.0)
                if p == 1:
                    part = part + attn[n, :, at].astype(jnp.float32)
                attn[n, :, at] = part.astype(BF)
            return total + jnp.sum(weights.reshape(16, 8, 640), axis=0)

        total = lax.fori_loop(0, 8, one, jnp.zeros((8, 640), jnp.float32))
        total = jnp.sum(total, axis=0, keepdims=True)
        for n in range(2):
            part = jnp.where(prompt == n, total, 0.0)
            mass[n, h : h + 1, :] = part + mass[n, h : h + 1, :] if p == 1 else part

    def attend_late():
        @pl.when(final_pair)
        def _():
            cache[1] = jnp.zeros((4, 512, 128), BF)
            valid[1] = jnp.zeros((8, 128), jnp.int32)

            @pl.when(c == 1)
            def _():
                kept = keeps[first, 8:16, :]
                valid[1] = jnp.where(kept >= 512, 1, 0)
                for h in range(2):
                    for k in range(4):
                        cache[1, k, h * 256 : (h + 1) * 256, :] = dot(
                            late[0, h * 256 : (h + 1) * 256, :], picker(kept[h * 4 + k : h * 4 + k + 1] - 512, 128)
                        ).astype(BF)

            for h in range(2):
                attend(1, h, late.at[c])

    lead(1)
    for k in range(4):
        for way, _ in WAYS:
            chunk_copy(way, 1, k).start()

    def hand_in(o):
        arrive(metas, r_me, o)
        took(tab.at[o, 4], r_c4.at[o])
        hand_out(o)

    def hand(way, s):
        return lambda: hand_in(origin(way, s))

    hand_out(z)
    receive(1, [lambda: attend(0, 0, spans.at[i])])
    receive(2, [hand("up", 1), hand("down", 1), lambda: attend(0, 1, spans.at[i])])
    receive(3, [hand("up", 2), hand("down", 2), attend_late])
    receive(4, [hand("up", 3), hand("down", 3)])
    hand_in(origin("up", 4))

    for copy in waits:
        copy.wait_send()
    for k in range(1, 8):
        @pl.when(z + k < 8)
        def _():
            marks_copy(k).wait_send()
            own_copy(k).wait_send()

    @pl.when(c == 1)
    def _():
        for copy in span_copies():
            copy.wait_send()

    @pl.when(final_pair)
    def _():
        late_copy().wait_send()

    for s in (1, 2, 3, 4):
        passed(s)

    for s, way in ((0, "up"), (1, "up"), (1, "down"), (2, "up"), (2, "down"), (3, "up"), (3, "down"), (4, "up")):
        o = origin(way, s)
        keep_local(o).wait()
        took(obuf.at[o, :, pl.ds(0, 496), :], s_ex.at[o])
        took(recv.at[pl.ds(0, 2), pl.ds(0, 496), :], r_ex.at[o])
        rows = pl.ds(pl.multiple_of(o * 64, 64), 64)
        for b in range(16):
            owned[rows, b * 128 : (b + 1) * 128] = recv[b, rows, :]


def whole(offsets, kv, q, keep, dest):
    V, D = pltpu.VMEM, pltpu.SemaphoreType.DMA
    vmem = pl.BlockSpec(memory_space=V)
    return pl.pallas_call(
        kernel,
        out_shape=(
            jax.ShapeDtypeStruct((2, 128, 2048), BF),
            jax.ShapeDtypeStruct((2, 2, 640), jnp.float32),
            jax.ShapeDtypeStruct((512, 2048), BF),
        ),
        in_specs=[pl.BlockSpec(memory_space=pltpu.SMEM)] + [vmem] * 4,
        out_specs=(vmem,) * 3,
        scratch_shapes=[
            V((16, 512, 128), BF),
            V((8, 512, 128), BF),
            V((8, 16, 128), jnp.int32),
            V((8, 64, 128), BF),
            V((2, 8, 128), jnp.int32),
            V((256, 128), BF),
            V((8, 256, 128), BF),
            V((8, 8, 128), jnp.int32),
            V((8, 256, 128), BF),
            V((2, 512, 128), BF),
            V((2, 4, 512, 128), BF),
            V((2, 8, 128), jnp.int32),
            V((8, 5, 256, 128), BF),
            V((8, 16, 128), jnp.int32),
            V((2, 256, 128), BF),
            V((8, 2, 512, 128), BF),
        ]
        + [D((8,))] * 10
        + [D] * 2
        + [D((25,))] * 4
        + [D] * 4
        + [D((8,))] * 8
        + [D((16,))]
        + [D] * 2,
        compiler_params=pltpu.CompilerParams(collective_id=0, has_side_effects=True, vmem_limit_bytes=40 << 20),
    )(offsets, kv, q, keep, dest)


def tiled(rows):
    prompts, count, width = rows.shape
    return jnp.transpose(rows.reshape(prompts, count // 8, 8, width // 128, 128), (0, 1, 3, 2, 4))


def local(query, kv_rows, keep, dest, offsets):
    return whole(
        offsets,
        tiled(kv_rows),
        tiled(query),
        keep[:, 0],
        dest.reshape(8, 128),
    )


def solution(mesh):
    placed = (
        P(None, "ctx", "kv"),
        P(None, "ctx", "kv"),
        P(None, "ctx", "kv", None),
        P("ctx", None),
        P(),
    )
    return jax.shard_map(
        local,
        mesh=mesh,
        in_specs=placed,
        out_specs=(P(None, "ctx", "kv"), P(None, "kv", "ctx"), P(("ctx", "kv"), None)),
        check_vma=False,
    )
```

```python
import math

import jax
import jax.numpy as jnp
from jax import lax
from jax.experimental import pallas as pl
from jax.experimental.pallas import tpu as pltpu
from jax.sharding import PartitionSpec as P

MESH = pl.DeviceIdType.MESH
BF = jnp.bfloat16
HEAD = 128


def lookup(table, index):
    row = lax.broadcasted_iota(jnp.int32, (8, 128), 0)
    lane = jnp.bitwise_and(index, 127)
    part = jnp.right_shift(index, 7)
    out = jnp.zeros_like(table)
    for k in range(4):
        low = jnp.broadcast_to(table[k : k + 1], (8, 128))
        high = jnp.broadcast_to(table[4 + k : 5 + k], (8, 128))
        spread = jnp.where(row < 4, low, high)
        found = jnp.take_along_axis(spread, lane, axis=1, mode="promise_in_bounds")
        out = jnp.where(part == k, found, out)
    return out


def picker(index, count):
    rows = lax.broadcasted_iota(jnp.int32, (count, index.shape[1]), 0)
    return jnp.where(rows == index, 1.0, 0.0).astype(BF)


def dot(a, b):
    return jnp.dot(a, b, preferred_element_type=jnp.float32)


def dot_t(a, b):
    return lax.dot_general(a, b, (((1,), (1,)), ((), ())), preferred_element_type=jnp.float32)


def flat(rows):
    return jnp.concatenate([rows[k : k + 1] for k in range(4)], axis=1)


def lanes(parts):
    return jnp.concatenate(parts, axis=1)


def inverse(kept, values):
    row = lax.broadcasted_iota(jnp.int32, (16, 128), 0)
    total = jnp.zeros((16, 640), jnp.float32)
    for k in range(4):
        value = values[k : k + 1] + 1
        high = jnp.broadcast_to(jnp.right_shift(value, 6), (16, 128))
        low = jnp.broadcast_to(jnp.bitwise_and(value, 63), (16, 128))
        digits = jnp.where(row == 0, high, jnp.where(row == 1, low, 0)).astype(jnp.float32).astype(BF)
        total = total + dot_t(digits, picker(kept[k : k + 1], 640))
    return (total[0:1] * 64.0 + total[1:2]).astype(jnp.int32) - 1


def half(rows, which):
    return jnp.where(which == 0, rows[0:4], rows[4:8])


def kernel(offs, kv, query, keep, dest, attn, mass, owned, recv, q, spans, keeps, units, goals, own, owns, marks, cz, late, cache, valid, tab, metas, tabl, obuf,
           s_sp, s_ke, s_ow, s_ma, s_cz, r_sp, r_ke, r_ow, r_ma, r_cz, s_la, r_la,
           s_up, r_up, s_dn, r_dn, s_lu, r_lu, s_ld, r_ld, s_ex, r_ex, s_lo, s_un, r_un, s_me, r_me, s_go, r_go, s_q):
    j = lax.axis_index("ctx")
    x = lax.axis_index("kv")
    z = j // 8
    i = lax.rem(j, 8)
    y = i // 2
    c = lax.rem(i, 2)
    me = i * 4 + x
    early = jnp.where(offs[0] == 0, 0, 1)

    def zdev(n):
        return (n * 8 + i, x)

    def pdev(n):
        return (z * 8 + n, x)

    def mdev(n):
        return (z * 8 + n // 4, lax.rem(n, 4))

    barrier = pltpu.get_barrier_semaphore()

    @pl.loop(1, 32)
    def _(k):
        pl.semaphore_signal(barrier, inc=1, device_id=mdev(lax.rem(me + k, 32)), device_id_type=MESH)

    @pl.loop(1, 8)
    def _(k):
        pl.semaphore_signal(barrier, inc=1, device_id=zdev(lax.rem(z + k, 8)), device_id_type=MESH)

    for p in range(2):
        lists = keep[early if p == 0 else 1 - early]
        for h in range(2):
            for k in range(4):
                at = p * 8 + h * 4 + k
                keeps[i, at : at + 1, :] = lists[h : h + 1, k * 128 : (k + 1) * 128]
    for b in range(4):
        spans[i, b * 128 : (b + 1) * 128, :] = kv[early, :, b].reshape(128, 128).T
    pltpu.make_async_copy(query, q, s_q).start()
    final_pair = j >= 62

    @pl.when(final_pair)
    def _():
        for b in range(4):
            late[c, b * 128 : (b + 1) * 128, :] = kv[1 - early, :, b].reshape(128, 128).T

    cols = pl.ds(pl.multiple_of(i * 64, 64), 64)
    units[i] = spans[i, cols, :]
    pl.semaphore_wait(barrier, 38)

    def send(src, dst, ss, rs, dev):
        return pltpu.make_async_remote_copy(
            src_ref=src, dst_ref=dst, send_sem=ss, recv_sem=rs, device_id=dev, device_id_type=MESH
        )

    def took(view, sem):
        pltpu.make_async_copy(view, view, sem).wait()

    def arrive(buf, sem, k):
        took(buf.at[k], sem.at[k])

    def late_copy():
        return send(late.at[c], late.at[c], s_la, r_la, pdev(7 - c))

    waits = []
    for k in range(1, 8):
        copy = send(keeps.at[i], keeps.at[i], s_ke.at[k], r_ke.at[i], pdev(lax.rem(i + k, 8)))
        copy.start()
        waits.append(copy)
    for k in range(1, 8):
        n = lax.rem(i + k, 8)
        copy = send(spans.at[i, pl.ds(pl.multiple_of(n * 64, 64), 64), :], units.at[i], s_un.at[k], r_un.at[i], pdev(n))
        copy.start()
        waits.append(copy)
    for k in range(1, 8):
        copy = send(spans.at[i], spans.at[i], s_sp.at[k], r_sp.at[i], pdev(lax.rem(i + k, 8)))
        copy.start()
        waits.append(copy)

    @pl.when(final_pair)
    def _():
        late_copy().start()

    for k in range(1, 8):
        arrive(keeps, r_ke, lax.rem(i + k, 8))
    slot = lax.rem(lax.broadcasted_iota(jnp.int32, (8, 128), 0), 4) * 128 + lax.broadcasted_iota(jnp.int32, (8, 128), 1)
    pre, mine = slot, slot
    for n in range(8):
        mine = jnp.where(i == n, pre, mine)
        kept = keeps[n, 0:8, :]
        pre = jnp.where(kept < 512, lookup(pre, jnp.minimum(kept, 511)), kept + 128 * n)
    marks[z] = pre

    def marks_copy(k):
        return send(marks.at[z], marks.at[z], s_ma.at[k], r_ma.at[z], zdev(z + k))

    def own_copy(k):
        return send(own, owns.at[z], s_ow.at[k], r_ow.at[z], zdev(z + k))

    for k in range(1, 8):
        @pl.when(z + k < 8)
        def _():
            marks_copy(k).start()

    for k in range(1, 8):
        arrive(units, r_un, lax.rem(i + k, 8))
    head = jnp.where(i < 4, pre[0:4], pre[4:8])
    unit = lanes([units[n] for n in range(8)])
    picked = dot(unit, picker(flat(head) - 512, 1024)).astype(BF)
    for k in range(4):
        own[k * 64 : (k + 1) * 64, :] = picked[:, k * 128 : (k + 1) * 128]
    for k in range(1, 8):
        @pl.when(z + k < 8)
        def _():
            own_copy(k).start()

    owners = dest[...]
    side = lax.broadcasted_iota(jnp.int32, (128, 128), 0) < lax.broadcasted_iota(jnp.int32, (128, 128), 1)
    earlier = jnp.where(side, 1.0, 0.0).astype(BF)
    count = jnp.zeros((256, 1), jnp.float32)
    for n in range(8):
        named = picker(owners[n : n + 1], 256)
        before = dot(named, earlier) + count
        named = named.astype(jnp.float32)
        rank = jnp.sum(named * before, axis=0, keepdims=True)
        count = count + jnp.sum(named, axis=1, keepdims=True)
        goals[c, n : n + 1, :] = owners[n : n + 1] * 8 + rank.astype(jnp.int32)
    first, second = i - c, i - c + 1
    copy = send(goals.at[c], goals.at[c], s_go, r_go, pdev(first + 1 - c))
    copy.start()
    waits.append(copy)

    for k in range(1, 8):
        arrive(spans, r_sp, lax.rem(i + k, 8))
    for h in range(2):
        table = lanes([spans[n, h * 256 : (h + 1) * 256, :] for n in range(8)])
        picked = dot(table, picker(flat(mine[h * 4 : h * 4 + 4]) - 512, 1024)).astype(BF)
        for k in range(4):
            cache[0, k, h * 256 : (h + 1) * 256, :] = picked[:, k * 128 : (k + 1) * 128]

    took(goals.at[1 - c], r_go)
    goal0 = half(goals[0], early)
    goal1 = inverse(half(keeps[second, 0:8, :], c), half(goals[1], early))
    metas[z, 0:4, :] = goal0
    metas[z, 4:8, :] = jnp.full((4, 128), -1, jnp.int32)
    for k in range(5):
        metas[z, 8 + k : 9 + k, :] = goal1[:, k * 128 : (k + 1) * 128]
    metas[z, 13:16, :] = jnp.full((3, 128), -1, jnp.int32)

    @pl.when(final_pair)
    def _():
        kept0 = half(keeps[first, 8:16, :], c)
        kept1 = half(keeps[second, 8:16, :], c)
        out1 = inverse(kept1, half(goals[1], 1 - early))
        back = jnp.concatenate([out1[:, k * 128 : (k + 1) * 128] for k in range(4)], axis=0)
        metas[z, 5:6, :] = inverse(kept0, half(goals[0], 1 - early))[:, 512:640]
        metas[z, 13:14, :] = inverse(kept0, back)[:, 512:640]
        metas[z, 14:15, :] = out1[:, 512:640]

    for k in range(1, 8):
        copy = send(metas.at[z], metas.at[z], s_me.at[k], r_me.at[z], zdev(lax.rem(z + k, 8)))
        copy.start()
        waits.append(copy)

    own_tokens = lax.broadcasted_iota(jnp.int32, (128, 128), 1) <= lax.broadcasted_iota(jnp.int32, (128, 128), 0)

    def attend(p, h, span_t, low=0, high=8):
        def chunk(at):
            return lanes([cache[p, k, at : at + 128, :] for k in range(4)] + [span_t[at : at + 128, :]])

        keys, values = chunk(h * 256), chunk(h * 256 + 128)
        seen = lanes([jnp.broadcast_to(valid[p, h * 4 + k : h * 4 + k + 1, :], (128, 128)) for k in range(4)]) > 0
        near = own_tokens
        prompt = early if p == 0 else 1 - early
        scale = 1.0 / math.sqrt(HEAD)

        def one(g, total):
            scores = dot(q[prompt, :, h * 8 + g].reshape(128, 128), keys) * scale
            old = jnp.where(seen, scores[:, 0:512], -1e30)
            new = jnp.where(near, scores[:, 512:640], -1e30)
            peak = jnp.maximum(jnp.max(old, axis=1, keepdims=True), jnp.max(new, axis=1, keepdims=True))
            expo = lanes([jnp.where(seen, jnp.exp(old - peak), 0.0), jnp.where(near, jnp.exp(new - peak), 0.0)])
            weights = expo * (1.0 / jnp.sum(expo, axis=1, keepdims=True))
            mixed = dot_t(weights.astype(BF), values)
            at = pl.ds(pl.multiple_of((h * 8 + g) * 128, 128), 128)
            for n in range(2):
                part = jnp.where(prompt == n, mixed, 0.0)
                attn[n, :, at] = (part + attn[n, :, at].astype(jnp.float32)).astype(BF)
            return total + jnp.sum(weights.reshape(16, 8, 640), axis=0)

        total = lax.fori_loop(low, high, one, jnp.zeros((8, 640), jnp.float32))
        total = jnp.sum(total, axis=0, keepdims=True)
        for n in range(2):
            mass[n, h : h + 1, :] += jnp.where(prompt == n, total, 0.0)

    def late_cache():
        attn[...] = jnp.zeros((2, 128, 2048), BF)
        mass[...] = jnp.zeros((2, 2, 640), jnp.float32)

        @pl.when(final_pair)
        def _():
            took(late.at[1 - c], r_la)
            for h in range(2):
                tabl[h] = late[h, pl.ds(pl.multiple_of(c * 256, 256), 256), :]
            cache[1] = jnp.zeros((4, 512, 128), BF)
            valid[1] = jnp.zeros((8, 128), jnp.int32)

            @pl.when(c == 1)
            def _():
                kept = keeps[first, 8:16, :]
                valid[1] = jnp.where(kept >= 512, 1, 0)
                for h in range(2):
                    for k in range(4):
                        cache[1, k, h * 256 : (h + 1) * 256, :] = dot(
                            late[0, h * 256 : (h + 1) * 256, :], picker(kept[h * 4 + k : h * 4 + k + 1] - 512, 128)
                        ).astype(BF)

    def attend_late(h):
        @pl.when(final_pair)
        def _():
            attend(1, h, late.at[c])

    late_cache()
    pltpu.make_async_copy(query, q, s_q).wait()
    attend_late(0)

    above, below = zdev(lax.rem(z + 1, 8)), zdev(lax.rem(z + 7, 8))

    WAYS = (("up", 1), ("down", -1))

    def chunks(way, s):
        return range(4) if s < 4 else (range(2) if way == "up" else range(2, 4))

    def origin(way, s):
        return lax.rem(z + 8 - s, 8) if way == "up" else lax.rem(z + s, 8)

    def chunk_copy(way, s, k):
        o = origin(way, s - 1)
        ss, rs, to = (s_up, r_up, above) if way == "up" else (s_dn, r_dn, below)
        return send(tab.at[o, k], tab.at[o, k], ss.at[s * 5 + k], rs.at[s * 5 + k], to)

    def tabl_copy(way):
        ss, rs, to = (s_lu, r_lu, above) if way == "up" else (s_ld, r_ld, below)
        return send(tabl, tabl, ss, rs, to)

    def goes(way, s):
        return s <= (4 if way == "up" else 3)

    def span_start():
        tab[z, 4] = spans[second, pl.ds(pl.multiple_of(c * 256, 256), 256), :]
        for way, _ in WAYS:
            chunk_copy(way, 1, 4).start()

    def span_next(s):
        for way, _ in WAYS:
            if goes(way, s):
                took(tab.at[origin(way, s), 4], (r_up if way == "up" else r_dn).at[s * 5 + 4])
            if goes(way, s + 1):
                chunk_copy(way, s + 1, 4).start()

    for n in range(7):
        @pl.when(n < z)
        def _():
            arrive(marks, r_ma, n)
    cur = jnp.full((8, 128), -1, jnp.int32)
    for n in range(7):
        m = jnp.where(n < z, marks[n], slot)
        new = jnp.where(m < 512, lookup(cur, jnp.minimum(m, 511)), n * 512 + slot)
        cur = jnp.where(n < z, new, cur)
    chead = jnp.where(i < 4, cur[0:4], cur[4:8])
    part = cz.at[i]
    part[...] = jnp.zeros((256, 128), BF)
    for n in range(7):
        @pl.when(n < z)
        def _():
            arrive(owns, r_ow, n)
            table = lanes([owns[n, p * 64 : (p + 1) * 64, :] for p in range(4)])
            picked = dot(table, picker(flat(chead) - n * 512, 512)).astype(BF)
            for k in range(4):
                part[k * 64 : (k + 1) * 64, :] += picked[:, k * 128 : (k + 1) * 128]
    for k in range(1, 8):
        copy = send(cz.at[i], cz.at[i], s_cz.at[k], r_cz.at[i], pdev(lax.rem(i + k, 8)))
        copy.start()
        waits.append(copy)

    span_start()
    was = jnp.where(cur >= 0, 1, 0)
    valid[0] = jnp.where(mine >= 512, 1, lookup(was, jnp.minimum(mine, 511)))

    span_next(1)
    attend_late(1)
    for k in range(1, 8):
        arrive(cz, r_cz, lax.rem(i + k, 8))
    span_next(2)
    for h in range(2):
        table = jnp.concatenate(
            [lanes([cz[n, p * 64 : (p + 1) * 64, :] for p in range(4)]) for n in range(h * 4, h * 4 + 4)], axis=0
        )
        picked = dot(table, picker(flat(mine[h * 4 : h * 4 + 4]), 512)).astype(BF)
        for k in range(4):
            cache[0, k, h * 256 : (h + 1) * 256, :] += picked[:, k * 128 : (k + 1) * 128]

    @pl.when(c == 1)
    def _():
        for k in range(4):
            tab[z, k] = cache[0, k, 256:512, :]

    @pl.when(c == 0)
    def _():
        table = lanes([cache[0, k, 0:256, :] for k in range(4)] + [spans[i, 0:256, :]])
        kept = keeps[i, 0:8, :]
        picked = dot(table, picker(flat(kept), 640)).astype(BF)
        for k in range(4):
            tab[z, k] = picked[:, k * 128 : (k + 1) * 128]

    def has_late(way, s):
        return (origin(way, s) == 7) & (y == 3)

    def lead(s):
        for way, _ in WAYS:
            if goes(way, s):
                @pl.when(has_late(way, s - 1))
                def _():
                    tabl_copy(way).start()

    def receive(s, tasks):
        for way, _ in WAYS:
            if goes(way, s):
                @pl.when(has_late(way, s))
                def _():
                    took(tabl, r_lu if way == "up" else r_ld)
        if s < 4:
            lead(s + 1)
        for task in tasks[:2]:
            task()
        for k in range(4):
            for way, _ in WAYS:
                if k in chunks(way, s):
                    took(tab.at[origin(way, s), k], (r_up if way == "up" else r_dn).at[s * 5 + k])
                if s < 4 and k in chunks(way, s + 1):
                    chunk_copy(way, s + 1, k).start()
            if k + 2 < len(tasks):
                tasks[k + 2]()

    def passed(s):
        for way, _ in WAYS:
            for k in chunks(way, s):
                chunk_copy(way, s, k).wait_send()
            if goes(way, s):
                chunk_copy(way, s, 4).wait_send()

                @pl.when(has_late(way, s - 1))
                def _():
                    tabl_copy(way).wait_send()

    def exchange(o, n):
        dst = recv.at[pl.ds(x * 4 + c * 2, 2), pl.ds(pl.multiple_of((o * 4 + y) * 16, 16), 16), :]
        return send(obuf.at[o, :, pl.ds(pl.multiple_of(n * 16, 16), 16), :], dst, s_ex.at[o], r_ex.at[o], mdev(n))

    def keep_local(o):
        dst = recv.at[pl.ds(x * 4 + c * 2, 2), pl.ds(pl.multiple_of((o * 4 + y) * 16, 16), 16), :]
        return pltpu.make_async_copy(obuf.at[o, :, pl.ds(pl.multiple_of(me * 16, 16), 16), :], dst, s_lo.at[o])

    line = lax.broadcasted_iota(jnp.int32, (512, 128), 0)
    place = z * 256 + jnp.right_shift(line, 4) * 8 + jnp.bitwise_and(line, 7)
    later = jnp.bitwise_and(line, 8) > 0

    def hit(o, k):
        wanted = jnp.where(later, metas[o, 8 + k : 9 + k, :], metas[o, k : k + 1, :])
        return jnp.where(wanted == place, 1.0, 0.0).astype(BF)

    def hand_out(o):
        rows = dot_t(lanes([hit(o, k) for k in range(5)]), lanes([tab[o, k] for k in range(5)])).astype(BF)
        obuf[o, 0] = rows[:, 0:128]
        obuf[o, 1] = rows[:, 128:256]

        @pl.when((o == 7) & (y == 3))
        def _():
            rows = dot_t(lanes([hit(o, k) for k in (5, 6)]), lanes([tabl[k] for k in range(2)])).astype(BF)
            obuf[o, 0] += rows[:, 0:128]
            obuf[o, 1] += rows[:, 128:256]

        @pl.loop(1, 32)
        def _(k):
            exchange(o, lax.rem(me + k, 32)).start()

        keep_local(o).start()

    lead(1)
    for k in range(4):
        for way, _ in WAYS:
            chunk_copy(way, 1, k).start()
    span_next(3)

    def hand_in(o):
        arrive(metas, r_me, o)
        hand_out(o)

    def hand(way, s):
        return lambda: hand_in(origin(way, s))

    hand_out(z)
    receive(1, [lambda: span_next(4), lambda: attend(0, 0, spans.at[i], 0, 3), lambda: attend(0, 0, spans.at[i], 3, 6)])
    receive(2, [hand("up", 1), hand("down", 1), lambda: attend(0, 0, spans.at[i], 6, 8), lambda: attend(0, 1, spans.at[i], 0, 2)])
    receive(3, [hand("up", 2), hand("down", 2), lambda: attend(0, 1, spans.at[i], 2, 5), lambda: attend(0, 1, spans.at[i], 5, 8)])
    receive(4, [hand("up", 3), hand("down", 3)])
    hand_in(origin("up", 4))

    for copy in waits:
        copy.wait_send()
    for k in range(1, 8):
        @pl.when(z + k < 8)
        def _():
            marks_copy(k).wait_send()
            own_copy(k).wait_send()

    @pl.when(final_pair)
    def _():
        late_copy().wait_send()

    for s in (1, 2, 3, 4):
        passed(s)

    for s, way in ((0, "up"), (1, "up"), (1, "down"), (2, "up"), (2, "down"), (3, "up"), (3, "down"), (4, "up")):
        o = origin(way, s)
        keep_local(o).wait()
        took(obuf.at[o, :, pl.ds(0, 496), :], s_ex.at[o])
        took(recv.at[pl.ds(0, 2), pl.ds(0, 496), :], r_ex.at[o])
        rows = pl.ds(pl.multiple_of(o * 64, 64), 64)
        for b in range(16):
            owned[rows, b * 128 : (b + 1) * 128] = recv[b, rows, :]


def whole(offsets, kv, q, keep, dest):
    V, D = pltpu.VMEM, pltpu.SemaphoreType.DMA
    vmem = pl.BlockSpec(memory_space=V)
    return pl.pallas_call(
        kernel,
        out_shape=(
            jax.ShapeDtypeStruct((2, 128, 2048), BF),
            jax.ShapeDtypeStruct((2, 2, 640), jnp.float32),
            jax.ShapeDtypeStruct((512, 2048), BF),
        ),
        in_specs=[pl.BlockSpec(memory_space=pltpu.SMEM), vmem, pl.BlockSpec(memory_space=pl.ANY), vmem, vmem],
        out_specs=(vmem,) * 3,
        scratch_shapes=[
            V((16, 512, 128), BF),
            V((2, 16, 16, 8, 128), BF),
            V((8, 512, 128), BF),
            V((8, 16, 128), jnp.int32),
            V((8, 64, 128), BF),
            V((2, 8, 128), jnp.int32),
            V((256, 128), BF),
            V((8, 256, 128), BF),
            V((8, 8, 128), jnp.int32),
            V((8, 256, 128), BF),
            V((2, 512, 128), BF),
            V((2, 4, 512, 128), BF),
            V((2, 8, 128), jnp.int32),
            V((8, 5, 256, 128), BF),
            V((8, 16, 128), jnp.int32),
            V((2, 256, 128), BF),
            V((8, 2, 512, 128), BF),
        ]
        + [D((8,))] * 10
        + [D] * 2
        + [D((25,))] * 4
        + [D] * 4
        + [D((8,))] * 7
        + [D] * 3,
        compiler_params=pltpu.CompilerParams(collective_id=0, has_side_effects=True, vmem_limit_bytes=40 << 20),
    )(offsets, kv, q, keep, dest)


def tiled(rows):
    prompts, count, width = rows.shape
    return jnp.transpose(rows.reshape(prompts, count // 8, 8, width // 128, 128), (0, 1, 3, 2, 4))


def local(query, kv_rows, keep, dest, offsets):
    return whole(
        offsets,
        tiled(kv_rows),
        tiled(query),
        keep[:, 0],
        dest.reshape(8, 128),
    )


def solution(mesh):
    placed = (
        P(None, "ctx", "kv"),
        P(None, "ctx", "kv"),
        P(None, "ctx", "kv", None),
        P("ctx", None),
        P(),
    )
    return jax.shard_map(
        local,
        mesh=mesh,
        in_specs=placed,
        out_specs=(P(None, "ctx", "kv"), P(None, "kv", "ctx"), P(("ctx", "kv"), None)),
        check_vma=False,
    )
```

```python
import math

import jax
import jax.numpy as jnp
from jax import lax
from jax.experimental import pallas as pl
from jax.experimental.pallas import tpu as pltpu
from jax.sharding import PartitionSpec as P

MESH = pl.DeviceIdType.MESH
BF = jnp.bfloat16
HEAD = 128


def lookup(table, index):
    row = lax.broadcasted_iota(jnp.int32, (8, 128), 0)
    lane = jnp.bitwise_and(index, 127)
    part = jnp.right_shift(index, 7)
    out = jnp.zeros_like(table)
    for k in range(4):
        low = jnp.broadcast_to(table[k : k + 1], (8, 128))
        high = jnp.broadcast_to(table[4 + k : 5 + k], (8, 128))
        spread = jnp.where(row < 4, low, high)
        found = jnp.take_along_axis(spread, lane, axis=1, mode="promise_in_bounds")
        out = jnp.where(part == k, found, out)
    return out


def picker(index, count):
    rows = lax.broadcasted_iota(jnp.int32, (count, index.shape[1]), 0)
    return jnp.where(rows == index, 1.0, 0.0).astype(BF)


def dot(a, b):
    return jnp.dot(a, b, preferred_element_type=jnp.float32)


def dot_t(a, b):
    return lax.dot_general(a, b, (((1,), (1,)), ((), ())), preferred_element_type=jnp.float32)


def flat(rows):
    return jnp.concatenate([rows[k : k + 1] for k in range(4)], axis=1)


def lanes(parts):
    return jnp.concatenate(parts, axis=1)


def inverse(kept, values):
    row = lax.broadcasted_iota(jnp.int32, (16, 128), 0)
    total = jnp.zeros((16, 640), jnp.float32)
    for k in range(4):
        value = values[k : k + 1] + 1
        high = jnp.broadcast_to(jnp.right_shift(value, 6), (16, 128))
        low = jnp.broadcast_to(jnp.bitwise_and(value, 63), (16, 128))
        digits = jnp.where(row == 0, high, jnp.where(row == 1, low, 0)).astype(jnp.float32).astype(BF)
        total = total + dot_t(digits, picker(kept[k : k + 1], 640))
    return (total[0:1] * 64.0 + total[1:2]).astype(jnp.int32) - 1


def half(rows, which):
    return jnp.where(which == 0, rows[0:4], rows[4:8])


def kernel(offs, kv, query, keep, dest, attn, mass, owned, recv, q, spans, keeps, units, goals, own, owns, marks, cz, late, cache, valid, tab, metas, tabl, obuf,
           s_sp, s_ke, s_ow, s_ma, s_cz, r_sp, r_ke, r_ow, r_ma, r_cz, s_la, r_la,
           s_up, r_up, s_dn, r_dn, s_lu, r_lu, s_ld, r_ld, s_ex, r_ex, s_lo, s_un, r_un, s_me, r_me, s_go, r_go, s_q):
    j = lax.axis_index("ctx")
    x = lax.axis_index("kv")
    z = j // 8
    i = lax.rem(j, 8)
    y = i // 2
    c = lax.rem(i, 2)
    me = i * 4 + x
    early = jnp.where(offs[0] == 0, 0, 1)

    def zdev(n):
        return (n * 8 + i, x)

    def pdev(n):
        return (z * 8 + n, x)

    def mdev(n):
        return (z * 8 + n // 4, lax.rem(n, 4))

    barrier = pltpu.get_barrier_semaphore()

    @pl.loop(1, 32)
    def _(k):
        pl.semaphore_signal(barrier, inc=1, device_id=mdev(lax.rem(me + k, 32)), device_id_type=MESH)

    @pl.loop(1, 8)
    def _(k):
        pl.semaphore_signal(barrier, inc=1, device_id=zdev(lax.rem(z + k, 8)), device_id_type=MESH)

    for p in range(2):
        lists = keep[early if p == 0 else 1 - early]
        for h in range(2):
            for k in range(4):
                at = p * 8 + h * 4 + k
                keeps[i, at : at + 1, :] = lists[h : h + 1, k * 128 : (k + 1) * 128]
    for b in range(4):
        spans[i, b * 128 : (b + 1) * 128, :] = kv[early, :, b].reshape(128, 128).T
    pltpu.make_async_copy(query, q, s_q).start()
    final_pair = j >= 62

    @pl.when(final_pair)
    def _():
        for b in range(4):
            late[c, b * 128 : (b + 1) * 128, :] = kv[1 - early, :, b].reshape(128, 128).T

    cols = pl.ds(pl.multiple_of(i * 64, 64), 64)
    units[i] = spans[i, cols, :]
    pl.semaphore_wait(barrier, 38)

    def send(src, dst, ss, rs, dev):
        return pltpu.make_async_remote_copy(
            src_ref=src, dst_ref=dst, send_sem=ss, recv_sem=rs, device_id=dev, device_id_type=MESH
        )

    def took(view, sem):
        pltpu.make_async_copy(view, view, sem).wait()

    def arrive(buf, sem, k):
        took(buf.at[k], sem.at[k])

    def late_copy():
        return send(late.at[c], late.at[c], s_la, r_la, pdev(7 - c))

    waits = []
    for k in range(1, 8):
        copy = send(keeps.at[i], keeps.at[i], s_ke.at[k], r_ke.at[i], pdev(lax.rem(i + k, 8)))
        copy.start()
        waits.append(copy)
    for k in range(1, 8):
        n = lax.rem(i + k, 8)
        copy = send(spans.at[i, pl.ds(pl.multiple_of(n * 64, 64), 64), :], units.at[i], s_un.at[k], r_un.at[i], pdev(n))
        copy.start()
        waits.append(copy)
    for k in range(1, 8):
        copy = send(spans.at[i], spans.at[i], s_sp.at[k], r_sp.at[i], pdev(lax.rem(i + k, 8)))
        copy.start()
        waits.append(copy)

    @pl.when(final_pair)
    def _():
        late_copy().start()

    for k in range(1, 8):
        arrive(keeps, r_ke, lax.rem(i + k, 8))
    slot = lax.rem(lax.broadcasted_iota(jnp.int32, (8, 128), 0), 4) * 128 + lax.broadcasted_iota(jnp.int32, (8, 128), 1)
    pre, mine = slot, slot
    for n in range(8):
        mine = jnp.where(i == n, pre, mine)
        kept = keeps[n, 0:8, :]
        pre = jnp.where(kept < 512, lookup(pre, jnp.minimum(kept, 511)), kept + 128 * n)
    marks[z] = pre

    def marks_copy(k):
        return send(marks.at[z], marks.at[z], s_ma.at[k], r_ma.at[z], zdev(z + k))

    def own_copy(k):
        return send(own, owns.at[z], s_ow.at[k], r_ow.at[z], zdev(z + k))

    for k in range(1, 8):
        @pl.when(z + k < 8)
        def _():
            marks_copy(k).start()

    for k in range(1, 8):
        arrive(units, r_un, lax.rem(i + k, 8))
    head = jnp.where(i < 4, pre[0:4], pre[4:8])
    unit = lanes([units[n] for n in range(8)])
    picked = dot(unit, picker(flat(head) - 512, 1024)).astype(BF)
    for k in range(4):
        own[k * 64 : (k + 1) * 64, :] = picked[:, k * 128 : (k + 1) * 128]
    for k in range(1, 8):
        @pl.when(z + k < 8)
        def _():
            own_copy(k).start()

    owners = dest[...]
    side = lax.broadcasted_iota(jnp.int32, (128, 128), 0) < lax.broadcasted_iota(jnp.int32, (128, 128), 1)
    earlier = jnp.where(side, 1.0, 0.0).astype(BF)
    count = jnp.zeros((256, 1), jnp.float32)
    for n in range(8):
        named = picker(owners[n : n + 1], 256)
        before = dot(named, earlier) + count
        named = named.astype(jnp.float32)
        rank = jnp.sum(named * before, axis=0, keepdims=True)
        count = count + jnp.sum(named, axis=1, keepdims=True)
        goals[c, n : n + 1, :] = owners[n : n + 1] * 8 + rank.astype(jnp.int32)
    first, second = i - c, i - c + 1
    copy = send(goals.at[c], goals.at[c], s_go, r_go, pdev(first + 1 - c))
    copy.start()
    waits.append(copy)

    for k in range(1, 8):
        arrive(spans, r_sp, lax.rem(i + k, 8))
    for h in range(2):
        table = lanes([spans[n, h * 256 : (h + 1) * 256, :] for n in range(8)])
        picked = dot(table, picker(flat(mine[h * 4 : h * 4 + 4]) - 512, 1024)).astype(BF)
        for k in range(4):
            cache[0, k, h * 256 : (h + 1) * 256, :] = picked[:, k * 128 : (k + 1) * 128]

    took(goals.at[1 - c], r_go)
    goal0 = half(goals[0], early)
    goal1 = inverse(half(keeps[second, 0:8, :], c), half(goals[1], early))
    metas[z, 0:4, :] = goal0
    metas[z, 4:8, :] = jnp.full((4, 128), -1, jnp.int32)
    for k in range(5):
        metas[z, 8 + k : 9 + k, :] = goal1[:, k * 128 : (k + 1) * 128]
    metas[z, 13:16, :] = jnp.full((3, 128), -1, jnp.int32)

    @pl.when(final_pair)
    def _():
        kept0 = half(keeps[first, 8:16, :], c)
        kept1 = half(keeps[second, 8:16, :], c)
        out1 = inverse(kept1, half(goals[1], 1 - early))
        back = jnp.concatenate([out1[:, k * 128 : (k + 1) * 128] for k in range(4)], axis=0)
        metas[z, 5:6, :] = inverse(kept0, half(goals[0], 1 - early))[:, 512:640]
        metas[z, 13:14, :] = inverse(kept0, back)[:, 512:640]
        metas[z, 14:15, :] = out1[:, 512:640]

    for k in range(1, 8):
        copy = send(metas.at[z], metas.at[z], s_me.at[k], r_me.at[z], zdev(lax.rem(z + k, 8)))
        copy.start()
        waits.append(copy)

    own_tokens = lax.broadcasted_iota(jnp.int32, (128, 128), 1) <= lax.broadcasted_iota(jnp.int32, (128, 128), 0)

    def attend(p, h, span_t, low=0, high=8):
        def chunk(at):
            return lanes([cache[p, k, at : at + 128, :] for k in range(4)] + [span_t[at : at + 128, :]])

        keys, values = chunk(h * 256), chunk(h * 256 + 128)
        seen = lanes([jnp.broadcast_to(valid[p, h * 4 + k : h * 4 + k + 1, :], (128, 128)) for k in range(4)]) > 0
        near = own_tokens
        prompt = early if p == 0 else 1 - early
        scale = 1.0 / math.sqrt(HEAD)

        def one(g, total):
            scores = dot(q[prompt, :, h * 8 + g].reshape(128, 128), keys) * scale
            old = jnp.where(seen, scores[:, 0:512], -1e30)
            new = jnp.where(near, scores[:, 512:640], -1e30)
            peak = jnp.maximum(jnp.max(old, axis=1, keepdims=True), jnp.max(new, axis=1, keepdims=True))
            expo = lanes([jnp.where(seen, jnp.exp(old - peak), 0.0), jnp.where(near, jnp.exp(new - peak), 0.0)])
            weights = expo * (1.0 / jnp.sum(expo, axis=1, keepdims=True))
            mixed = dot_t(weights.astype(BF), values)
            at = pl.ds(pl.multiple_of((h * 8 + g) * 128, 128), 128)
            for n in range(2):
                part = jnp.where(prompt == n, mixed, 0.0)
                attn[n, :, at] = (part + attn[n, :, at].astype(jnp.float32)).astype(BF)
            return total + jnp.sum(weights.reshape(16, 8, 640), axis=0)

        total = lax.fori_loop(low, high, one, jnp.zeros((8, 640), jnp.float32))
        total = jnp.sum(total, axis=0, keepdims=True)
        for n in range(2):
            mass[n, h : h + 1, :] += jnp.where(prompt == n, total, 0.0)

    def late_cache():
        attn[...] = jnp.zeros((2, 128, 2048), BF)
        mass[...] = jnp.zeros((2, 2, 640), jnp.float32)

        @pl.when(final_pair)
        def _():
            took(late.at[1 - c], r_la)
            for h in range(2):
                tabl[h] = late[h, pl.ds(pl.multiple_of(c * 256, 256), 256), :]
            cache[1] = jnp.zeros((4, 512, 128), BF)
            valid[1] = jnp.zeros((8, 128), jnp.int32)

            @pl.when(c == 1)
            def _():
                kept = keeps[first, 8:16, :]
                valid[1] = jnp.where(kept >= 512, 1, 0)
                for h in range(2):
                    for k in range(4):
                        cache[1, k, h * 256 : (h + 1) * 256, :] = dot(
                            late[0, h * 256 : (h + 1) * 256, :], picker(kept[h * 4 + k : h * 4 + k + 1] - 512, 128)
                        ).astype(BF)

    def attend_late(h):
        @pl.when(final_pair)
        def _():
            attend(1, h, late.at[c])

    late_cache()
    pltpu.make_async_copy(query, q, s_q).wait()
    attend_late(0)

    above, below = zdev(lax.rem(z + 1, 8)), zdev(lax.rem(z + 7, 8))

    WAYS = (("up", 1), ("down", -1))

    def chunks(way, s):
        return range(4) if s < 4 else (range(2) if way == "up" else range(2, 4))

    def origin(way, s):
        return lax.rem(z + 8 - s, 8) if way == "up" else lax.rem(z + s, 8)

    def chunk_copy(way, s, k):
        o = origin(way, s - 1)
        ss, rs, to = (s_up, r_up, above) if way == "up" else (s_dn, r_dn, below)
        return send(tab.at[o, k], tab.at[o, k], ss.at[s * 5 + k], rs.at[s * 5 + k], to)

    def tabl_copy(way):
        ss, rs, to = (s_lu, r_lu, above) if way == "up" else (s_ld, r_ld, below)
        return send(tabl, tabl, ss, rs, to)

    def goes(way, s):
        return s <= (4 if way == "up" else 3)

    def span_start():
        tab[z, 4] = spans[second, pl.ds(pl.multiple_of(c * 256, 256), 256), :]
        for way, _ in WAYS:
            chunk_copy(way, 1, 4).start()

    def span_next(s):
        for way, _ in WAYS:
            if goes(way, s):
                took(tab.at[origin(way, s), 4], (r_up if way == "up" else r_dn).at[s * 5 + 4])
            if goes(way, s + 1):
                chunk_copy(way, s + 1, 4).start()

    for n in range(7):
        @pl.when(n < z)
        def _():
            arrive(marks, r_ma, n)
    cur = jnp.full((8, 128), -1, jnp.int32)
    for n in range(7):
        m = jnp.where(n < z, marks[n], slot)
        new = jnp.where(m < 512, lookup(cur, jnp.minimum(m, 511)), n * 512 + slot)
        cur = jnp.where(n < z, new, cur)
    chead = jnp.where(i < 4, cur[0:4], cur[4:8])
    part = cz.at[i]
    part[...] = jnp.zeros((256, 128), BF)
    for n in range(7):
        @pl.when(n < z)
        def _():
            arrive(owns, r_ow, n)
            table = lanes([owns[n, p * 64 : (p + 1) * 64, :] for p in range(4)])
            picked = dot(table, picker(flat(chead) - n * 512, 512)).astype(BF)
            for k in range(4):
                part[k * 64 : (k + 1) * 64, :] += picked[:, k * 128 : (k + 1) * 128]
    for k in range(1, 8):
        copy = send(cz.at[i], cz.at[i], s_cz.at[k], r_cz.at[i], pdev(lax.rem(i + k, 8)))
        copy.start()
        waits.append(copy)

    span_start()
    was = jnp.where(cur >= 0, 1, 0)
    valid[0] = jnp.where(mine >= 512, 1, lookup(was, jnp.minimum(mine, 511)))

    span_next(1)
    attend_late(1)
    for k in range(1, 8):
        arrive(cz, r_cz, lax.rem(i + k, 8))
    span_next(2)
    for h in range(2):
        table = jnp.concatenate(
            [lanes([cz[n, p * 64 : (p + 1) * 64, :] for p in range(4)]) for n in range(h * 4, h * 4 + 4)], axis=0
        )
        picked = dot(table, picker(flat(mine[h * 4 : h * 4 + 4]), 512)).astype(BF)
        for k in range(4):
            cache[0, k, h * 256 : (h + 1) * 256, :] += picked[:, k * 128 : (k + 1) * 128]

    @pl.when(c == 1)
    def _():
        for k in range(4):
            tab[z, k] = cache[0, k, 256:512, :]

    @pl.when(c == 0)
    def _():
        table = lanes([cache[0, k, 0:256, :] for k in range(4)] + [spans[i, 0:256, :]])
        kept = keeps[i, 0:8, :]
        picked = dot(table, picker(flat(kept), 640)).astype(BF)
        for k in range(4):
            tab[z, k] = picked[:, k * 128 : (k + 1) * 128]

    def has_late(way, s):
        return (origin(way, s) == 7) & (y == 3)

    def lead(s):
        for way, _ in WAYS:
            if goes(way, s):
                @pl.when(has_late(way, s - 1))
                def _():
                    tabl_copy(way).start()

    def receive(s, tasks):
        for way, _ in WAYS:
            if goes(way, s):
                @pl.when(has_late(way, s))
                def _():
                    took(tabl, r_lu if way == "up" else r_ld)
        if s < 4:
            lead(s + 1)
        for task in tasks[:2]:
            task()
        for k in range(4):
            for way, _ in WAYS:
                if k in chunks(way, s):
                    took(tab.at[origin(way, s), k], (r_up if way == "up" else r_dn).at[s * 5 + k])
                if s < 4 and k in chunks(way, s + 1):
                    chunk_copy(way, s + 1, k).start()
            if k + 2 < len(tasks):
                tasks[k + 2]()

    def passed(s):
        for way, _ in WAYS:
            for k in chunks(way, s):
                chunk_copy(way, s, k).wait_send()
            if goes(way, s):
                chunk_copy(way, s, 4).wait_send()

                @pl.when(has_late(way, s - 1))
                def _():
                    tabl_copy(way).wait_send()

    def exchange(o, n, m):
        dst = recv.at[pl.ds(x * 4 + c * 2, 2), pl.ds(pl.multiple_of((o * 4 + y) * 16, 16), 16), :]
        return send(obuf.at[o, :, pl.ds(pl.multiple_of((n * 4 + m) * 16, 16), 16), :], dst, s_ex.at[o], r_ex.at[o], (z * 8 + n, m))

    def keep_local(o):
        dst = recv.at[pl.ds(x * 4 + c * 2, 2), pl.ds(pl.multiple_of((o * 4 + y) * 16, 16), 16), :]
        return pltpu.make_async_copy(obuf.at[o, :, pl.ds(pl.multiple_of(me * 16, 16), 16), :], dst, s_lo.at[o])

    line = lax.broadcasted_iota(jnp.int32, (512, 128), 0)
    place = z * 256 + jnp.right_shift(line, 4) * 8 + jnp.bitwise_and(line, 7)
    later = jnp.bitwise_and(line, 8) > 0

    def hit(o, k):
        wanted = jnp.where(later, metas[o, 8 + k : 9 + k, :], metas[o, k : k + 1, :])
        return jnp.where(wanted == place, 1.0, 0.0).astype(BF)

    def hand_out(o):
        rows = dot_t(lanes([hit(o, k) for k in range(5)]), lanes([tab[o, k] for k in range(5)])).astype(BF)
        obuf[o, 0] = rows[:, 0:128]
        obuf[o, 1] = rows[:, 128:256]

        @pl.when((o == 7) & (y == 3))
        def _():
            rows = dot_t(lanes([hit(o, k) for k in (5, 6)]), lanes([tabl[k] for k in range(2)])).astype(BF)
            obuf[o, 0] += rows[:, 0:128]
            obuf[o, 1] += rows[:, 128:256]

        for d in range(1, 4):
            exchange(o, i, lax.rem(x + d, 4)).start()

        @pl.loop(1, 8)
        def _(k):
            n = lax.rem(i + k, 8)
            for d in range(4):
                exchange(o, n, lax.rem(x + d, 4)).start()

        keep_local(o).start()

    lead(1)
    for k in range(4):
        for way, _ in WAYS:
            chunk_copy(way, 1, k).start()
    span_next(3)

    def hand_in(o):
        arrive(metas, r_me, o)
        hand_out(o)

    def hand(way, s):
        return lambda: hand_in(origin(way, s))

    hand_out(z)
    receive(1, [lambda: span_next(4), lambda: attend(0, 0, spans.at[i], 0, 3), lambda: attend(0, 0, spans.at[i], 3, 6)])
    receive(2, [hand("up", 1), hand("down", 1), lambda: attend(0, 0, spans.at[i], 6, 8), lambda: attend(0, 1, spans.at[i], 0, 2)])
    receive(3, [hand("up", 2), hand("down", 2), lambda: attend(0, 1, spans.at[i], 2, 5), lambda: attend(0, 1, spans.at[i], 5, 8)])
    receive(4, [hand("up", 3), hand("down", 3)])
    hand_in(origin("up", 4))

    for copy in waits:
        copy.wait_send()
    for k in range(1, 8):
        @pl.when(z + k < 8)
        def _():
            marks_copy(k).wait_send()
            own_copy(k).wait_send()

    @pl.when(final_pair)
    def _():
        late_copy().wait_send()

    for s in (1, 2, 3, 4):
        passed(s)

    for s, way in ((0, "up"), (1, "up"), (1, "down"), (2, "up"), (2, "down"), (3, "up"), (3, "down"), (4, "up")):
        o = origin(way, s)
        keep_local(o).wait()
        took(obuf.at[o, :, pl.ds(0, 496), :], s_ex.at[o])
        took(recv.at[pl.ds(0, 2), pl.ds(0, 496), :], r_ex.at[o])
        rows = pl.ds(pl.multiple_of(o * 64, 64), 64)
        for b in range(16):
            owned[rows, b * 128 : (b + 1) * 128] = recv[b, rows, :]


def whole(offsets, kv, q, keep, dest):
    V, D = pltpu.VMEM, pltpu.SemaphoreType.DMA
    vmem = pl.BlockSpec(memory_space=V)
    return pl.pallas_call(
        kernel,
        out_shape=(
            jax.ShapeDtypeStruct((2, 128, 2048), BF),
            jax.ShapeDtypeStruct((2, 2, 640), jnp.float32),
            jax.ShapeDtypeStruct((512, 2048), BF),
        ),
        in_specs=[pl.BlockSpec(memory_space=pltpu.SMEM), vmem, pl.BlockSpec(memory_space=pl.ANY), vmem, vmem],
        out_specs=(vmem,) * 3,
        scratch_shapes=[
            V((16, 512, 128), BF),
            V((2, 16, 16, 8, 128), BF),
            V((8, 512, 128), BF),
            V((8, 16, 128), jnp.int32),
            V((8, 64, 128), BF),
            V((2, 8, 128), jnp.int32),
            V((256, 128), BF),
            V((8, 256, 128), BF),
            V((8, 8, 128), jnp.int32),
            V((8, 256, 128), BF),
            V((2, 512, 128), BF),
            V((2, 4, 512, 128), BF),
            V((2, 8, 128), jnp.int32),
            V((8, 5, 256, 128), BF),
            V((8, 16, 128), jnp.int32),
            V((2, 256, 128), BF),
            V((8, 2, 512, 128), BF),
        ]
        + [D((8,))] * 10
        + [D] * 2
        + [D((25,))] * 4
        + [D] * 4
        + [D((8,))] * 7
        + [D] * 3,
        compiler_params=pltpu.CompilerParams(collective_id=0, has_side_effects=True, vmem_limit_bytes=40 << 20),
    )(offsets, kv, q, keep, dest)


def tiled(rows):
    prompts, count, width = rows.shape
    return jnp.transpose(rows.reshape(prompts, count // 8, 8, width // 128, 128), (0, 1, 3, 2, 4))


def local(query, kv_rows, keep, dest, offsets):
    return whole(
        offsets,
        tiled(kv_rows),
        tiled(query),
        keep[:, 0],
        dest.reshape(8, 128),
    )


def solution(mesh):
    placed = (
        P(None, "ctx", "kv"),
        P(None, "ctx", "kv"),
        P(None, "ctx", "kv", None),
        P("ctx", None),
        P(),
    )
    return jax.shard_map(
        local,
        mesh=mesh,
        in_specs=placed,
        out_specs=(P(None, "ctx", "kv"), P(None, "kv", "ctx"), P(("ctx", "kv"), None)),
        check_vma=False,
    )
```
